512 devices in a mesh: section: 16 (over z), seq: 32 (over y, x, core).
Axes of the slice: x: 4, y: 4, z: 16, core: 2. Of those that a mesh axis runs over, the one named last changes fastest.
Arguments:
- in_flight: bfloat16 [16, 2, 64, 4096], P('section', None, 'seq'), may hold values from -64 to 64
- entering: bfloat16 [3, 2, 64, 4096], P(None, None, 'seq'), may hold values from -64 to 64
- patch_frames: int32 [4], replicated, may hold values from 1 to 2, 6 in all
- norm_gain: bfloat16 [16, 4096], P('section'), may hold values from 0.5 to 1.5
- qkv_weight: bfloat16 [16, 4096, 3, 4096], P('section', None, None, 'seq'), may hold values from -0.15625 to 0.15625
- out_weight: bfloat16 [16, 4096, 4096], P('section', None, 'seq'), may hold values from -0.1875 to 0.1875
- stale_kv: bfloat16 [16, 4, 2, 64, 2, 4096], P('section', None, None, None, None, 'seq'), may hold values from -256 to 256
Outputs:
- hidden_out: bfloat16 [16, 4, 2, 64, 4096], P('section', None, None, 'seq')
The draws below stay inside these ranges and needn't reach their ends.
Inputs may be any that keep to these rules, and one draw needn't show every extreme that they name: `patch_frames`: the frames of the patches sum to 6 and the largest is exactly 2; frame slots past a patch's count in in_flight, entering and stale_kv are ignored.
All inputs are finite; a program needn't handle non-finite values.
Results may differ from the reference program's by a relative error of at most 0.039.
Values may be sent and summed in bfloat16 or wider, within the bound.
No kernel may reach another device: no remote copies, remote signals or barrier semaphores. Data moves between devices by JAX's collectives and lax.ppermute only.
A program may use at most 64 MiB of HBM per device.

```python
import math
import jax
import jax.numpy as jnp
import numpy as np
from jax import lax

HEADS = 32
HDIM = 128
PATCHES = 4
MOST = 2
FRAMES = 6
TPF = 64
D = 4096
LAYERS = 16


def scale_state(key, base_values):
    row_key, column_key = jax.random.split(key, 2)
    row_dims = base_values.shape[:-1] + (1,)
    width = base_values.shape[-1]
    row_scale = jnp.exp(jax.random.uniform(row_key, row_dims, jnp.float32, math.log(0.3), math.log(3.0)))
    column_scale = jnp.exp(jax.random.uniform(column_key, (width,), jnp.float32, math.log(0.3), math.log(3.0)))
    return (base_values * row_scale * column_scale).astype(jnp.bfloat16)


def draw_in_flight(key, part):
    key = jax.random.fold_in(key, 11)
    value_key, scale_key = jax.random.split(key)
    array_dims = (LAYERS, MOST, TPF, D)
    base_values = jnp.clip(jax.random.normal(value_key, array_dims, jnp.float32), -3.0, 3.0)
    return scale_state(scale_key, base_values)


def draw_entering(key, part):
    key = jax.random.fold_in(key, 12)
    value_key, scale_key = jax.random.split(key)
    array_dims = (PATCHES - 1, MOST, TPF, D)
    base_values = jnp.clip(jax.random.normal(value_key, array_dims, jnp.float32), -3.0, 3.0)
    return scale_state(scale_key, base_values)


def draw_stale_kv(key, part):
    key = jax.random.fold_in(key, 13)
    subkeys = jax.random.split(key, 1)
    array_dims = (LAYERS, PATCHES, MOST, TPF, 2, D)
    base_values = jnp.clip(jax.random.normal(subkeys[0], array_dims, jnp.float32), -4.0, 4.0) * 1.7
    return base_values.astype(jnp.bfloat16)


def block_levels(own_key, extent, pieces, low, high):
    def one(dim, shards_of):
        steps = jax.random.uniform(jax.random.fold_in(jax.random.fold_in(own_key, 6), dim), (shards_of,), jnp.float32, low / len(pieces), high / len(pieces))
        return jnp.repeat(jnp.exp(steps), extent[dim] // shards_of).reshape((-1,) + (1,) * (len(extent) - dim - 1))

    level = one(*pieces[0])
    for cut in pieces[1:]:
        level = level * one(*cut)
    return level


def length_profile(number_of, total, bound, lean):
    weights = [(1 << 20) // math.isqrt(rank ** lean) + 1 for rank in range(2, number_of + 1)]
    surplus, holding = total - bound - (number_of - 1), [1] * (number_of - 1)
    while surplus > 0:
        movable = [i for i in range(number_of - 1) if holding[i] < bound]
        whole, budget = sum([weights[i] for i in movable]), surplus
        for i in movable:
            addition = min(bound - holding[i], max(1, budget * weights[i] // whole), surplus)
            holding[i] = holding[i] + addition
            surplus = surplus - addition
    return np.array([bound] + holding)


def uneven(rng, number_of, total, most, slope):
    if number_of == 2:
        one = jax.random.randint(rng, (), max(1, total - most), min(most, total - 1) + 1)
        return jnp.stack([one, total - one])
    tallies = jnp.asarray(length_profile(number_of, total, most, slope), jnp.int32)
    couples = (number_of - 1) // 2
    source_of, receiver = tallies[1:1 + 2 * couples:2], tallies[2:2 + 2 * couples:2]
    slack = jnp.minimum(source_of - 1, most - receiver)
    shifted = jax.random.randint(jax.random.fold_in(rng, 1), (couples,), 0, 1 << 20) % (slack + 1)
    tallies = tallies.at[1:1 + 2 * couples:2].set(source_of - shifted).at[2:2 + 2 * couples:2].set(receiver + shifted)
    return tallies[jax.random.permutation(jax.random.fold_in(rng, 2), number_of)]


def scatter_about(own_key, shape, spread, limit, cuts=(), kind=jnp.bfloat16):
    entries = spread * jax.random.normal(own_key, shape, jnp.float32)
    if cuts:
        entries = entries * block_levels(own_key, shape, cuts, -0.22, 0.18)
    return jnp.clip(entries, -limit, limit).astype(kind)


def setup_inputs(seed: int = 0) -> dict:
    arg_keys = jax.random.split(jax.random.key(seed), 8)
    return {
        "in_flight": draw_in_flight(jax.random.fold_in(arg_keys[7], 71), 0),
        "entering": draw_entering(jax.random.fold_in(arg_keys[7], 71), 0),
        "patch_frames": uneven(arg_keys[2], PATCHES, FRAMES, MOST, 1).astype(jnp.int32),
        "norm_gain": jnp.clip(1.0 + 0.1 * jax.random.normal(arg_keys[3], (LAYERS, D), jnp.float32), 0.5, 1.5).astype(jnp.bfloat16),
        "qkv_weight": scatter_about(arg_keys[4], (LAYERS, D, 3, D), (D // 3) ** -0.5, 0.15625, ((0, 16), (3, 32))),
        "out_weight": scatter_about(arg_keys[5], (LAYERS, D, D), (D // 4) ** -0.5, 0.1875, ((0, 16), (2, 32))),
        "stale_kv": draw_stale_kv(jax.random.fold_in(arg_keys[7], 71), 0),
    }


def attend_heads(normed, patch_slot, buffer, weights_in, weights_out, key_live):
    flat_rows = normed.reshape(MOST * TPF, D)
    projected = jnp.dot(flat_rows, weights_in.reshape(D, 3 * D), preferred_element_type=jnp.float32)
    projected = lax.optimization_barrier(projected.astype(jnp.bfloat16)).reshape(MOST, TPF, 3, D)
    queries = projected[:, :, 0, :].reshape(MOST * TPF, HEADS, HDIM)
    new_slot = projected[:, :, 1:3, :]
    anchor = jnp.zeros((), jnp.int32)
    buffer = lax.dynamic_update_slice(buffer, new_slot[None], (patch_slot, anchor, anchor, anchor, anchor))
    keys_all = buffer[:, :, :, 0, :].reshape(PATCHES * MOST * TPF, HEADS, HDIM)
    values_all = buffer[:, :, :, 1, :].reshape(PATCHES * MOST * TPF, HEADS, HDIM)
    scores = jnp.einsum('qhd,khd->hqk', queries.astype(jnp.float32), keys_all.astype(jnp.float32)) / math.sqrt(HDIM)
    scores = jnp.where(key_live[None, None, :], scores, -jnp.inf)
    row_max = lax.optimization_barrier(jnp.max(scores, axis=2, keepdims=True))
    exponent = jnp.exp(scores - row_max)
    row_total = lax.optimization_barrier(jnp.sum(exponent, axis=2, keepdims=True))
    weights_low = lax.optimization_barrier(exponent.astype(jnp.bfloat16))
    attended = jnp.einsum('hqk,khd->qhd', weights_low.astype(jnp.float32), values_all.astype(jnp.float32))
    attended = attended / jnp.transpose(row_total, (1, 0, 2))
    attended = lax.optimization_barrier(attended.astype(jnp.bfloat16)).reshape(MOST * TPF, D)
    branch = jnp.dot(attended, weights_out, preferred_element_type=jnp.float32)
    branch = lax.optimization_barrier(branch.astype(jnp.bfloat16))
    return (branch.reshape(MOST, TPF, D), buffer)

def reference(in_flight, entering, patch_frames, norm_gain, qkv_weight, out_weight, stale_kv):
    frame_ids = jnp.arange(MOST, dtype=jnp.int32)
    live_table = frame_ids[None, :] < patch_frames[:, None]
    key_live = jnp.broadcast_to(live_table[:, :, None], (PATCHES, MOST, TPF)).reshape(PATCHES * MOST * TPF)
    anchor = jnp.zeros((), jnp.int32)

    def layer(previous, inputs):
        layer_index, first_input, gain_row, weights_in, weights_out, buffer = inputs
        results = []
        outputs = jnp.zeros((PATCHES, MOST, TPF, D), jnp.bfloat16)
        for tick_index in range(PATCHES):
            patch_slot = jnp.mod(tick_index - layer_index, PATCHES).astype(jnp.int32)
            if tick_index == 0:
                arrived = first_input
            else:
                arrived = jnp.where(layer_index == 0, entering[tick_index - 1], previous[tick_index - 1])
            live_rows = live_table[patch_slot]
            hidden = jnp.where(live_rows[:, None, None], arrived, jnp.zeros_like(arrived))
            widened = hidden.astype(jnp.float32)
            mean_square = lax.optimization_barrier(jnp.mean(widened * widened, axis=-1, keepdims=True))
            normed = (widened * lax.rsqrt(mean_square + 1e-06) * gain_row.astype(jnp.float32)).astype(jnp.bfloat16)
            branch, buffer = attend_heads(normed, patch_slot, buffer, weights_in, weights_out, key_live)
            result = jnp.where(live_rows[:, None, None], widened + branch.astype(jnp.float32), 0.0).astype(jnp.bfloat16)
            results.append(result)
            outputs = lax.dynamic_update_slice(outputs, result[None], (patch_slot, anchor, anchor, anchor))
        return (jnp.stack(results), outputs)
    layer_ids = jnp.arange(LAYERS, dtype=jnp.int32)
    start_state = jnp.zeros((PATCHES, MOST, TPF, D), jnp.bfloat16)
    last_layer, hidden_out = lax.scan(layer, start_state, (layer_ids, in_flight, norm_gain, qkv_weight, out_weight, stale_kv))
    return hidden_out
```

```python
import functools
import math

import jax
import jax.numpy as jnp
from jax import lax
from jax.experimental import pallas as pl
from jax.experimental.pallas import tpu as pltpu
from jax.sharding import PartitionSpec as P

HDIM = 128
CORES = 2
SPARE = 16
VMEM_LIMIT = 12 * 1024 * 1024


def call(body, name, out_shape, scalars, arrays, scratch=()):
    in_vmem = pl.BlockSpec(memory_space=pltpu.VMEM)
    in_smem = pl.BlockSpec(memory_space=pltpu.SMEM)
    return pl.pallas_call(
        body,
        out_shape=out_shape,
        in_specs=[in_smem] * len(scalars) + [in_vmem] * len(arrays),
        out_specs=jax.tree.map(lambda _: in_vmem, out_shape),
        scratch_shapes=list(scratch),
        compiler_params=pltpu.CompilerParams(vmem_limit_bytes=VMEM_LIMIT),
        name=name,
    )(*scalars, *arrays)


def shape(*dims):
    return jax.ShapeDtypeStruct(dims, jnp.bfloat16)


def join_weights(w_ref, out_ref):
    kinds, _, width = w_ref.shape
    for kind in range(kinds):
        out_ref[:, kind * width:(kind + 1) * width] = w_ref[kind]


def pack_first(mine_ref, later_ref, out_ref):
    rows = mine_ref.shape[0]
    for target in range(out_ref.shape[0]):
        out_ref[target, :rows] = mine_ref[...]
        out_ref[target, rows:] = later_ref[target]


def unpack_first(local, came_ref, hidden_ref, fresh_ref, wide_ref):
    group, rows, _ = came_ref.shape
    chips, frames, halves = hidden_ref.shape[:3]
    blocks = chips * halves
    for source in range(group):
        wide_ref[source * rows:(source + 1) * rows] = came_ref[source].astype(jnp.float32)

    def over_sources(row):
        return wide_ref[pl.ds(row, group, stride=rows), :].astype(jnp.bfloat16)

    for frame in range(frames):
        for t in range(local):
            for block in range(blocks):
                hidden_ref[block // halves, frame, block % halves, t * group:(t + 1) * group] = over_sources(
                    (frame * local + t) * blocks + block
                )
    for tick in range(fresh_ref.shape[0]):
        for t in range(local):
            for half in range(halves):
                fresh_ref[tick, half, t * group:(t + 1) * group] = over_sources(
                    frames * local * blocks + (tick * local + t) * halves + half
                )


def layer_front(info_ref, x_ref, gain_ref, w_ref, k_ref, v_ref, out_ref, k_out, v_out, xn_ref):
    chips, frames, halves, tokens, width = x_ref.shape
    slots = k_ref.shape[0]
    rows = frames * tokens
    slot = info_ref[slots]
    count = info_ref[slot]
    for frame in range(frames):
        squares = jnp.zeros((tokens, width), jnp.float32)
        for chip in range(chips):
            for half in range(halves):
                wide = x_ref[chip, frame, half].astype(jnp.float32)
                squares = squares + wide * wide
        mean_square = jnp.sum(squares, axis=1, keepdims=True) / (chips * halves * width)
        scale = jnp.where(frame < count, lax.rsqrt(mean_square + 1e-06), 0.0)
        for chip in range(chips):
            for half in range(halves):
                first = (chip * halves + half) * width
                wide = x_ref[chip, frame, half].astype(jnp.float32)
                normed = wide * scale * gain_ref[:, first:first + width].astype(jnp.float32)
                xn_ref[frame * tokens:(frame + 1) * tokens, first:first + width] = normed.astype(jnp.bfloat16)
    projected = jnp.dot(xn_ref[...], w_ref[...], preferred_element_type=jnp.float32).astype(jnp.bfloat16)
    queries = projected[:, :width]
    k_out[...] = k_ref[...]
    v_out[...] = v_ref[...]
    k_out[slot] = projected[:, width:2 * width]
    v_out[slot] = projected[:, 2 * width:]
    keys = k_out[...].reshape(slots * rows, width)
    values = v_out[...].reshape(slots * rows, width)
    scores = lax.dot_general(
        queries, keys, (((1,), (1,)), ((), ())), preferred_element_type=jnp.float32
    ) / math.sqrt(HDIM)
    key_ids = lax.broadcasted_iota(jnp.int32, (1, slots * rows), 1)
    key_slot = key_ids // rows
    limit = jnp.zeros_like(key_ids)
    for patch in range(slots):
        limit = jnp.where(key_slot == patch, info_ref[patch] * tokens, limit)
    scores = jnp.where(key_ids - key_slot * rows < limit, scores, -jnp.inf)
    exponent = jnp.exp(scores - jnp.max(scores, axis=1, keepdims=True))
    row_total = jnp.sum(exponent, axis=1, keepdims=True)
    attended = jnp.dot(exponent.astype(jnp.bfloat16), values, preferred_element_type=jnp.float32)
    attended = (attended / row_total).astype(jnp.bfloat16)
    for chip in range(chips):
        for frame in range(frames):
            out_ref[chip, frame] = attended[frame * tokens:(frame + 1) * tokens]


def layer_back(info_ref, a_ref, w_own_ref, w_other_ref, x_ref, out_ref, wide_ref):
    blocks, tokens, width = a_ref.shape
    slots = info_ref.shape[0] - 2
    me = info_ref[slots + 1]
    chip = lax.div(me, CORES)
    core = me - chip * CORES
    live = core < info_ref[info_ref[slots]]
    for block in range(blocks):
        wide_ref[:, block * width:(block + 1) * width] = a_ref[block]
    for half, w_ref in ((core, w_own_ref), (1 - core, w_other_ref)):
        branch = jnp.dot(wide_ref[...], w_ref[...], preferred_element_type=jnp.float32).astype(jnp.bfloat16)
        total = x_ref[chip, core, half].astype(jnp.float32) + branch.astype(jnp.float32)
        out_ref[half] = jnp.where(live, total, 0.0).astype(jnp.bfloat16)


def pack_last(*refs):
    *result_refs, out_ref, wide_ref = refs
    group, parts, _ = out_ref.shape
    each = parts // len(result_refs) * group
    for tick, ref in enumerate(result_refs):
        halves, tokens, width = ref.shape
        wide_ref[tick * each:(tick + 1) * each] = ref[...].astype(jnp.float32).reshape(halves * tokens, width)
    for target in range(group):
        out_ref[target] = wide_ref[pl.ds(target, parts, stride=group), :].astype(jnp.bfloat16)


def unpack_last(local, slots_ref, came_ref, out_ref, wide_ref, turn_ref):
    group, parts, _ = came_ref.shape
    patches = slots_ref.shape[0]
    chips = group // CORES
    for source in range(group):
        wide_ref[source * parts:(source + 1) * parts] = came_ref[source].astype(jnp.float32)
    for tick in range(patches):
        slot = slots_ref[tick]
        for frame in range(CORES):
            for t in range(local):
                for half in range(CORES):
                    part = (tick * CORES + half) * local + t
                    turn_ref[pl.ds(half, chips, stride=CORES), :] = wide_ref[
                        pl.ds(frame * parts + part, chips, stride=CORES * parts), :
                    ]
                out_ref[(slot * CORES + frame) * local + t] = turn_ref[...].astype(jnp.bfloat16)


def swap(value):
    return lax.all_to_all(value, "seq", split_axis=0, concat_axis=0, tiled=True)


def on_device(in_flight, entering, patch_frames, norm_gain, qkv_weight, out_weight, stale_kv):
    section = lax.axis_index("section")
    sections = lax.axis_size("section")
    me = lax.axis_index("seq")
    group = lax.axis_size("seq")
    patches, frames, tokens = stale_kv.shape[1:4]
    local = in_flight.shape[2]
    ticks = patches
    chips = group // CORES
    halves = CORES
    owned = frames * local * group
    hidden_dims = (chips, frames, halves, tokens, HDIM)
    w_own = out_weight[0]
    w_other = lax.ppermute(w_own, "seq", [(device, device ^ 1) for device in range(group)])
    keys = stale_kv[0, :, :, :, 0, :].reshape(patches, frames * tokens, HDIM)
    values = stale_kv[0, :, :, :, 1, :].reshape(patches, frames * tokens, HDIM)
    weights = call(
        join_weights, "join", shape(qkv_weight.shape[1], 3 * HDIM), (), (jnp.transpose(qkv_weight[0], (1, 0, 2)),)
    )

    mine = in_flight.reshape(owned, HDIM)
    later = entering.reshape(ticks - 1, frames, local, chips, halves, HDIM)
    later = jnp.transpose(later, (3, 1, 0, 2, 4, 5)).reshape(group, -1, HDIM)
    later = jnp.pad(later, ((0, 0), (0, SPARE - later.shape[1]), (0, 0)))
    came = swap(call(pack_first, "pack_first", shape(group, owned + SPARE, HDIM), (), (mine, later)))
    gathered, fresh = call(
        functools.partial(unpack_first, local),
        "unpack_first",
        (shape(*hidden_dims), shape(ticks - 1, halves, tokens, HDIM)),
        (),
        (came,),
        [pltpu.VMEM((group * (owned + SPARE), HDIM), jnp.float32)],
    )

    slots = jnp.mod(jnp.arange(ticks, dtype=jnp.int32) - section, patches).astype(jnp.int32)
    results = []
    for tick in range(ticks):
        info = jnp.concatenate([patch_frames, slots[tick:tick + 1], me.astype(jnp.int32).reshape(1)])
        if tick:
            arrived = lax.ppermute(
                results[-1], "section", [(source, source + 1) for source in range(sections - 1)]
            )
            arrived = jnp.where(section == 0, fresh[tick - 1], arrived)
            gathered = swap(jnp.broadcast_to(arrived[None], (group,) + arrived.shape)).reshape(hidden_dims)
        attended, keys, values = call(
            layer_front,
            "front",
            (shape(chips, frames, tokens, HDIM), shape(*keys.shape), shape(*values.shape)),
            (info,),
            (gathered, norm_gain, weights, keys, values),
            [pltpu.VMEM((frames * tokens, group * HDIM), jnp.bfloat16)],
        )
        attended = swap(attended.reshape(group, tokens, HDIM))
        results.append(
            call(
                layer_back,
                "back",
                shape(halves, tokens, HDIM),
                (info,),
                (attended, w_own, w_other, gathered),
                [pltpu.VMEM((tokens, group * HDIM), jnp.bfloat16)],
            )
        )

    parts = ticks * halves * local
    sent = call(
        pack_last,
        "pack_last",
        shape(group, parts, HDIM),
        (),
        tuple(results),
        [pltpu.VMEM((ticks * halves * tokens, HDIM), jnp.float32)],
    )
    outputs = call(
        functools.partial(unpack_last, local),
        "unpack_last",
        shape(patches * frames * local, group, HDIM),
        (slots,),
        (swap(sent),),
        [pltpu.VMEM((group * parts, HDIM), jnp.float32), pltpu.VMEM((group, HDIM), jnp.float32)],
    )
    return outputs.reshape(1, patches, frames, local, group * HDIM)


def solution(mesh):
    in_specs = (
        P("section", None, "seq", None),
        P(None, None, "seq", None),
        P(),
        P("section", None),
        P("section", None, None, "seq"),
        P("section", None, "seq"),
        P("section", None, None, None, None, "seq"),
    )
    out_specs = P("section", None, None, "seq", None)
    return jax.shard_map(
        on_device, mesh=mesh, in_specs=in_specs, out_specs=out_specs, check_vma=False
    )
```

```python
import functools
import math

import jax
import jax.numpy as jnp
from jax import lax
from jax.experimental import pallas as pl
from jax.experimental.pallas import tpu as pltpu
from jax.sharding import PartitionSpec as P

HDIM = 128
CORES = 2
MOST_SECTIONS = 1024
SPARE = 16
VMEM_LIMIT = 12 * 1024 * 1024


def call(body, name, out_shape, scalars, arrays, scratch=(), anywhere=()):
    in_vmem = pl.BlockSpec(memory_space=pltpu.VMEM)
    in_smem = pl.BlockSpec(memory_space=pltpu.SMEM)
    return pl.pallas_call(
        body,
        out_shape=out_shape,
        in_specs=[in_smem] * len(scalars)
        + [pl.BlockSpec(memory_space=pl.ANY) if place in anywhere else in_vmem for place in range(len(arrays))],
        out_specs=jax.tree.map(lambda _: in_vmem, out_shape),
        scratch_shapes=list(scratch),
        compiler_params=pltpu.CompilerParams(vmem_limit_bytes=VMEM_LIMIT),
        name=name,
    )(*scalars, *arrays)


def shape(*dims):
    return jax.ShapeDtypeStruct(dims, jnp.bfloat16)


def pack_first(mine_ref, later_ref, out_ref, rows_ref, spare_ref):
    _, frames, local, width = mine_ref.shape
    group = out_ref.shape[0]
    blocks = width // HDIM
    each = local * blocks
    for frame in range(frames):
        wide = mine_ref[0, frame].astype(jnp.float32)
        for block in range(blocks):
            rows_ref[pl.ds(frame * each + block, local, stride=blocks), :] = wide[:, block * HDIM:(block + 1) * HDIM]
    spare_ref[...] = jnp.zeros_like(spare_ref)
    for tick in range(later_ref.shape[0]):
        for frame in range(frames):
            wide = later_ref[tick, frame].astype(jnp.float32)
            for block in range(blocks):
                chip, half = divmod(block, CORES)
                row = (chip * CORES + frame) * SPARE + tick * local * CORES + half
                spare_ref[pl.ds(row, local, stride=CORES), :] = wide[:, block * HDIM:(block + 1) * HDIM]
    for target in range(group):
        frame = target % CORES
        out_ref[target, :each] = rows_ref[frame * each:(frame + 1) * each].astype(jnp.bfloat16)
        out_ref[target, each:] = spare_ref[target * SPARE:(target + 1) * SPARE].astype(jnp.bfloat16)


def side_by_side(core, wide, own_ref, other_ref, out_ref, sem_ref, first):
    copies = []
    for index, (ref, place) in enumerate(((own_ref, core), (other_ref, 1 - core))):
        columns = pl.ds(pl.multiple_of(place * wide + first, HDIM), HDIM)
        copies.append(pltpu.make_async_copy(ref, out_ref.at[:, columns], sem_ref.at[index]))
    return copies


def unpack_first(local, info_ref, came_ref, own_ref, other_ref, hidden_ref, fresh_ref, wkv_ref, wq_ref, wide_ref, sem_ref):
    group, rows, _ = came_ref.shape
    chips, halves = hidden_ref.shape[:2]
    blocks = chips * halves
    core = lax.rem(info_ref[info_ref.shape[0] - 1], CORES)
    copies = []
    for kind, (out_ref, wide, first) in enumerate(((wq_ref, HDIM, 0), (wkv_ref, 2 * HDIM, 0), (wkv_ref, 2 * HDIM, HDIM))):
        copies += side_by_side(core, wide, own_ref.at[kind], other_ref.at[kind], out_ref, sem_ref.at[kind], first)
    for copy in copies:
        copy.start()
    for source in range(group):
        wide_ref[source * rows:(source + 1) * rows] = came_ref[source].astype(jnp.float32)

    def over_sources(row):
        return wide_ref[pl.ds(row, group, stride=rows), :].astype(jnp.bfloat16)

    for t in range(local):
        for block in range(blocks):
            hidden_ref[block // halves, block % halves, t * group:(t + 1) * group] = over_sources(t * blocks + block)
    for tick in range(fresh_ref.shape[0]):
        for t in range(local):
            for half in range(halves):
                fresh_ref[tick, half, t * group:(t + 1) * group] = over_sources(
                    local * blocks + (tick * local + t) * halves + half
                )
    for copy in copies:
        copy.wait()


def join_out(info_ref, own_ref, other_ref, after_ref, out_ref, sem_ref):
    core = lax.rem(info_ref[info_ref.shape[0] - 1], CORES)
    copies = side_by_side(core, HDIM, own_ref, other_ref, out_ref, sem_ref, 0)
    for copy in copies:
        copy.start()
    for copy in copies:
        copy.wait()


def slot_of(info_ref, tick):
    slots = info_ref.shape[0] - 2
    return lax.rem(tick + slots * MOST_SECTIONS - info_ref[slots], slots)


def core_live(info_ref, tick):
    core = lax.rem(info_ref[info_ref.shape[0] - 1], CORES)
    return core < info_ref[slot_of(info_ref, tick)]


def layer_keys(tick, info_ref, x_ref, gain_ref, w_ref, *refs):
    *stale_ref, xn_ref, new_ref = refs
    chips, halves, tokens, width = x_ref.shape
    squares = jnp.zeros((tokens, width), jnp.float32)
    for chip in range(chips):
        for half in range(halves):
            wide = x_ref[chip, half].astype(jnp.float32)
            squares = squares + wide * wide
    mean_square = jnp.sum(squares, axis=1, keepdims=True) / (chips * halves * width)
    scale = jnp.where(core_live(info_ref, tick), lax.rsqrt(mean_square + 1e-06), 0.0)
    for chip in range(chips):
        for half in range(halves):
            first = (chip * halves + half) * width
            wide = x_ref[chip, half].astype(jnp.float32)
            normed = wide * scale * gain_ref[:, first:first + width].astype(jnp.float32)
            xn_ref[:, first:first + width] = normed.astype(jnp.bfloat16)
    new_ref[:tokens] = jnp.dot(xn_ref[...], w_ref[...], preferred_element_type=jnp.float32).astype(jnp.bfloat16)
    for ref in stale_ref:
        rows, both = ref.shape
        for part in range(CORES):
            new_ref[tokens:, part * both:(part + 1) * both] = ref[part * rows // CORES:(part + 1) * rows // CORES]


def layer_queries(xn_ref, w_ref, out_ref):
    out_ref[...] = jnp.dot(xn_ref[...], w_ref[...], preferred_element_type=jnp.float32).astype(jnp.bfloat16)


def layer_attend(tick, info_ref, q_ref, own_ref, other_ref, *refs):
    *kv_ref, out_ref, kv_out = refs
    chips, halves, tokens, width = out_ref.shape
    slots, frames = kv_out.shape[:2]
    rows = frames * tokens
    slot = slot_of(info_ref, tick)
    core = lax.rem(info_ref[slots + 1], CORES)
    for ref in kv_ref:
        kv_out[...] = ref[...]
    if not kv_ref:
        both = 2 * width
        dims = (slots // CORES, frames, tokens, both)
        for mine in range(CORES):

            @pl.when(core == mine)
            def _():
                for half, ref in enumerate((own_ref, other_ref) if mine == 0 else (other_ref, own_ref)):
                    for part in range(CORES):
                        kv_out[part * dims[0]:(part + 1) * dims[0], :, :, half * both:(half + 1) * both] = ref[
                            tokens:, part * both:(part + 1) * both
                        ].reshape(dims)

    kv_out[slot, core] = own_ref[:tokens]
    kv_out[slot, 1 - core] = other_ref[:tokens]
    key_ids = lax.broadcasted_iota(jnp.int32, (1, slots * rows), 1)
    key_slot = key_ids // rows
    limit = jnp.zeros_like(key_ids)
    for patch in range(slots):
        limit = jnp.where(key_slot == patch, info_ref[patch] * tokens, limit)
    key_live = key_ids - key_slot * rows < limit
    for half in range(halves):
        queries = q_ref[:, half * width:(half + 1) * width]
        keys = kv_out[:, :, :, 2 * half * width:(2 * half + 1) * width].reshape(slots * rows, width)
        values = kv_out[:, :, :, (2 * half + 1) * width:(2 * half + 2) * width].reshape(slots * rows, width)
        scores = lax.dot_general(
            queries, keys, (((1,), (1,)), ((), ())), preferred_element_type=jnp.float32
        ) / math.sqrt(HDIM)
        scores = jnp.where(key_live, scores, -jnp.inf)
        exponent = jnp.exp(scores - jnp.max(scores, axis=1, keepdims=True))
        row_total = jnp.sum(exponent, axis=1, keepdims=True)
        attended = jnp.dot(exponent.astype(jnp.bfloat16), values, preferred_element_type=jnp.float32)
        attended = (attended / row_total).astype(jnp.bfloat16)
        for chip in range(chips):
            out_ref[chip, half] = attended


def layer_back(tick, info_ref, a_ref, w_ref, x_ref, out_ref, wide_ref):
    chips, halves, tokens, width = a_ref.shape
    chip = lax.div(info_ref[info_ref.shape[0] - 1], CORES)
    live = core_live(info_ref, tick)
    for source in range(chips):
        for half in range(halves):
            first = (source * halves + half) * width
            wide_ref[:, first:first + width] = a_ref[source, half]
    branch = jnp.dot(wide_ref[...], w_ref[...], preferred_element_type=jnp.float32).astype(jnp.bfloat16)
    for half in range(halves):
        total = x_ref[chip, half].astype(jnp.float32) + branch[:, half * width:(half + 1) * width].astype(jnp.float32)
        out_ref[half] = jnp.where(live, total, 0.0).astype(jnp.bfloat16)


def pack_last(*refs):
    *result_refs, out_ref, wide_ref = refs
    group, parts, _ = out_ref.shape
    ticks = len(result_refs)
    for tick, ref in enumerate(result_refs):
        halves, tokens, _ = ref.shape
        for half in range(halves):
            first = (half * ticks + tick) * tokens
            wide_ref[first:first + tokens] = ref[half].astype(jnp.float32)
    for target in range(group):
        out_ref[target] = wide_ref[pl.ds(target, parts, stride=group), :].astype(jnp.bfloat16)


def unpack_last(info_ref, came_ref, out_ref, turn_ref):
    group, parts, width = came_ref.shape
    patches, frames, local, _ = out_ref.shape
    each = parts // CORES
    for source in range(group):
        chip, frame = divmod(source, CORES)
        wide = came_ref[source].astype(jnp.float32)
        for half in range(CORES):
            first = (chip * CORES + half) * width
            turn_ref[frame * each:(frame + 1) * each, first:first + width] = wide[half * each:(half + 1) * each]
    for tick in range(patches):
        slot = slot_of(info_ref, tick)
        for frame in range(frames):
            row = frame * each + tick * local
            out_ref[slot, frame] = turn_ref[row:row + local].astype(jnp.bfloat16)


def swap(value, groups=None):
    return lax.all_to_all(value, "seq", split_axis=0, concat_axis=0, tiled=True, axis_index_groups=groups)


def on_device(in_flight, entering, patch_frames, norm_gain, qkv_weight, out_weight, stale_kv):
    section = lax.axis_index("section")
    sections = lax.axis_size("section")
    me = lax.axis_index("seq")
    group = lax.axis_size("seq")
    patches, frames, tokens = stale_kv.shape[1:4]
    local = in_flight.shape[2]
    width = in_flight.shape[3]
    ticks = patches
    chips = group // CORES
    halves = CORES
    owned = local * group
    same_core = [[CORES * chip + core for chip in range(chips)] for core in range(CORES)]
    partner = [(device, device ^ 1) for device in range(group)]
    info = jnp.concatenate([patch_frames, jnp.stack([section, me]).astype(jnp.int32)])

    w_in = jnp.transpose(qkv_weight[0], (1, 0, 2))
    w_in_other = lax.ppermute(w_in, "seq", partner)
    sent = call(
        pack_first,
        "pack_first",
        shape(group, owned + SPARE, HDIM),
        (),
        (in_flight, entering),
        [pltpu.VMEM((frames * owned, HDIM), jnp.float32), pltpu.VMEM((group * SPARE, HDIM), jnp.float32)],
    )
    sent, w_out_own = lax.optimization_barrier((sent, out_weight[0]))
    came = swap(sent)
    w_out_other = lax.ppermute(w_out_own, "seq", partner)
    stale = stale_kv[0].reshape(patches * frames * tokens, 2 * HDIM)
    gathered, fresh, w_kv, w_q = call(
        functools.partial(unpack_first, local),
        "unpack_first",
        (
            shape(chips, halves, tokens, HDIM),
            shape(ticks - 1, halves, tokens, HDIM),
            shape(width, 2 * halves * HDIM),
            shape(width, halves * HDIM),
        ),
        (info,),
        (came, w_in, w_in_other),
        [pltpu.VMEM((group * (owned + SPARE), HDIM), jnp.float32), pltpu.SemaphoreType.DMA((3, CORES))],
        anywhere=(1, 2),
    )
    w_out = call(
        join_out,
        "join_out",
        shape(width, halves * HDIM),
        (info,),
        (out_weight[0], w_out_other, fresh),
        [pltpu.SemaphoreType.DMA((CORES,))],
        anywhere=(0, 1, 2),
    )

    new_rows = tokens + patches * frames * tokens // CORES
    results = []
    for tick in range(ticks):
        if tick:
            arrived = lax.ppermute(
                results[-1], "section", [(source, source + 1) for source in range(sections - 1)]
            )
            arrived = jnp.where(section == 0, fresh[tick - 1], arrived)
            gathered = swap(jnp.broadcast_to(arrived[None], (chips,) + arrived.shape), same_core)
        normed, own = call(
            functools.partial(layer_keys, tick),
            "keys",
            (shape(tokens, width), shape(tokens if tick else new_rows, 2 * halves * HDIM)),
            (info,),
            (gathered, norm_gain, w_kv) + (() if tick else (stale,)),
        )
        other = lax.ppermute(own, "seq", partner)
        queries = call(layer_queries, "queries", shape(tokens, halves * HDIM), (), (normed, w_q))
        attended, kv = call(
            functools.partial(layer_attend, tick),
            "attend",
            (shape(chips, halves, tokens, HDIM), shape(patches, frames, tokens, 2 * halves * HDIM)),
            (info,),
            (queries, own, other) + ((kv,) if tick else ()),
        )
        results.append(
            call(
                functools.partial(layer_back, tick),
                "back",
                shape(halves, tokens, HDIM),
                (info,),
                (swap(attended, same_core), w_out, gathered),
                [pltpu.VMEM((tokens, width), jnp.bfloat16)],
            )
        )

    parts = ticks * halves * local
    sent = call(
        pack_last,
        "pack_last",
        shape(group, parts, HDIM),
        (),
        tuple(results),
        [pltpu.VMEM((ticks * halves * tokens, HDIM), jnp.float32)],
    )
    outputs = call(
        unpack_last,
        "unpack_last",
        shape(patches, frames, local, width),
        (info,),
        (swap(sent),),
        [pltpu.VMEM((parts, width), jnp.float32)],
    )
    return outputs[None]


def solution(mesh):
    in_specs = (
        P("section", None, "seq", None),
        P(None, None, "seq", None),
        P(),
        P("section", None),
        P("section", None, None, "seq"),
        P("section", None, "seq"),
        P("section", None, None, None, None, "seq"),
    )
    out_specs = P("section", None, None, "seq", None)
    return jax.shard_map(
        on_device, mesh=mesh, in_specs=in_specs, out_specs=out_specs, check_vma=False
    )
```

```python
import functools
import math

import jax
import jax.numpy as jnp
from jax import lax
from jax.experimental import pallas as pl
from jax.experimental.pallas import tpu as pltpu
from jax.sharding import PartitionSpec as P

HDIM = 128
CORES = 2
MOST_SECTIONS = 1024
SPARE = 16
VMEM_LIMIT = 12 * 1024 * 1024


def call(body, name, out_shape, scalars, arrays, scratch=(), in_hbm=(), anywhere=(), out_specs=None):
    arrays = [
        pltpu.with_memory_space_constraint(array, pltpu.HBM) if place in in_hbm else array
        for place, array in enumerate(arrays)
    ]
    in_vmem = pl.BlockSpec(memory_space=pltpu.VMEM)
    in_smem = pl.BlockSpec(memory_space=pltpu.SMEM)
    return pl.pallas_call(
        body,
        out_shape=out_shape,
        in_specs=[in_smem] * len(scalars)
        + [pl.BlockSpec(memory_space=pl.ANY) if place in (*in_hbm, *anywhere) else in_vmem for place in range(len(arrays))],
        out_specs=jax.tree.map(lambda _: in_vmem, out_shape) if out_specs is None else out_specs,
        scratch_shapes=list(scratch),
        compiler_params=pltpu.CompilerParams(vmem_limit_bytes=VMEM_LIMIT),
        name=name,
    )(*scalars, *arrays)


def shape(*dims):
    return jax.ShapeDtypeStruct(dims, jnp.bfloat16)


def kept(*dims):
    return pltpu.VMEM(dims, jnp.bfloat16)


def pack_first(mine_any, later_any, out_ref, mine_ref, later_ref, rows_ref, spare_ref, sem_ref):
    _, frames, local, width = mine_ref.shape
    copies = [
        pltpu.make_async_copy(mine_any, mine_ref, sem_ref.at[0]),
        pltpu.make_async_copy(later_any, later_ref, sem_ref.at[1]),
    ]
    for copy in copies:
        copy.start()
    spare_ref[...] = jnp.zeros_like(spare_ref)
    for copy in copies:
        copy.wait()
    group = out_ref.shape[0]
    blocks = width // HDIM
    each = local * blocks
    for frame in range(frames):
        wide = mine_ref[0, frame].astype(jnp.float32)
        for block in range(blocks):
            rows_ref[pl.ds(frame * each + block, local, stride=blocks), :] = wide[:, block * HDIM:(block + 1) * HDIM]
    for tick in range(later_ref.shape[0]):
        for frame in range(frames):
            wide = later_ref[tick, frame].astype(jnp.float32)
            for block in range(blocks):
                chip, half = divmod(block, CORES)
                row = (chip * CORES + frame) * SPARE + tick * local * CORES + half
                spare_ref[pl.ds(row, local, stride=CORES), :] = wide[:, block * HDIM:(block + 1) * HDIM]
    for target in range(group):
        frame = target % CORES
        out_ref[target, :each] = rows_ref[frame * each:(frame + 1) * each].astype(jnp.bfloat16)
        out_ref[target, each:] = spare_ref[target * SPARE:(target + 1) * SPARE].astype(jnp.bfloat16)


def side_by_side(core, wide, own_ref, other_ref, out_ref, sem_ref, first):
    copies = []
    for index, (ref, place) in enumerate(((own_ref, core), (other_ref, 1 - core))):
        columns = pl.ds(pl.multiple_of(place * wide + first, HDIM), HDIM)
        copies.append(pltpu.make_async_copy(ref, out_ref.at[:, columns], sem_ref.at[index]))
    return copies


def unpack_first(
    local, info_ref, came_any, own_ref, other_ref,
    hidden_ref, fresh_ref, wkv_ref, wq_ref, came_ref, wide_ref, came_sem, sem_ref,
):
    group, rows, _ = came_ref.shape
    chips, halves = hidden_ref.shape[:2]
    blocks = chips * halves
    core = lax.rem(info_ref[info_ref.shape[0] - 1], CORES)
    first_copy = pltpu.make_async_copy(came_any, came_ref, came_sem.at[0])
    first_copy.start()
    copies = []
    for kind, (out_ref, wide, first) in enumerate(((wq_ref, HDIM, 0), (wkv_ref, 2 * HDIM, 0), (wkv_ref, 2 * HDIM, HDIM))):
        copies += side_by_side(core, wide, own_ref.at[kind], other_ref.at[kind], out_ref, sem_ref.at[kind], first)
    for copy in copies:
        copy.start()
    first_copy.wait()
    for source in range(group):
        wide_ref[source * rows:(source + 1) * rows] = came_ref[source].astype(jnp.float32)

    def over_sources(row):
        return wide_ref[pl.ds(row, group, stride=rows), :].astype(jnp.bfloat16)

    for t in range(local):
        for block in range(blocks):
            hidden_ref[block // halves, block % halves, t * group:(t + 1) * group] = over_sources(t * blocks + block)
    for tick in range(fresh_ref.shape[0]):
        for t in range(local):
            for half in range(halves):
                fresh_ref[tick, half, t * group:(t + 1) * group] = over_sources(
                    local * blocks + (tick * local + t) * halves + half
                )
    for copy in copies:
        copy.wait()


def slot_of(info_ref, tick):
    slots = info_ref.shape[0] - 2
    return lax.rem(tick + slots * MOST_SECTIONS - info_ref[slots], slots)


def core_live(info_ref, tick):
    core = lax.rem(info_ref[info_ref.shape[0] - 1], CORES)
    return core < info_ref[slot_of(info_ref, tick)]


def layer_keys(tick, info_ref, x_ref, gain_ref, w_ref, *refs):
    *stale_ref, xn_ref, new_ref = refs
    chips, halves, tokens, width = x_ref.shape
    squares = jnp.zeros((tokens, width), jnp.float32)
    for chip in range(chips):
        for half in range(halves):
            wide = x_ref[chip, half].astype(jnp.float32)
            squares = squares + wide * wide
    mean_square = jnp.sum(squares, axis=1, keepdims=True) / (chips * halves * width)
    scale = jnp.where(core_live(info_ref, tick), lax.rsqrt(mean_square + 1e-06), 0.0)
    for chip in range(chips):
        for half in range(halves):
            first = (chip * halves + half) * width
            wide = x_ref[chip, half].astype(jnp.float32)
            normed = wide * scale * gain_ref[:, first:first + width].astype(jnp.float32)
            xn_ref[:, first:first + width] = normed.astype(jnp.bfloat16)
    new_ref[:tokens] = jnp.dot(xn_ref[...], w_ref[...], preferred_element_type=jnp.float32).astype(jnp.bfloat16)
    for ref in stale_ref:
        rows, both = ref.shape
        for part in range(CORES):
            new_ref[tokens:, part * both:(part + 1) * both] = ref[part * rows // CORES:(part + 1) * rows // CORES]


def layer_queries(xn_ref, w_ref, out_ref):
    out_ref[...] = jnp.dot(xn_ref[...], w_ref[...], preferred_element_type=jnp.float32).astype(jnp.bfloat16)


def live_keys(info_ref, slots, rows, tokens):
    key_ids = lax.broadcasted_iota(jnp.int32, (1, slots * rows), 1)
    key_slot = key_ids // rows
    limit = jnp.zeros_like(key_ids)
    for patch in range(slots):
        limit = jnp.where(key_slot == patch, info_ref[patch] * tokens, limit)
    return key_ids, key_ids - key_slot * rows < limit


def softmax_part(queries, keys, values, live):
    scores = lax.dot_general(
        queries, keys, (((1,), (1,)), ((), ())), preferred_element_type=jnp.float32
    ) / math.sqrt(HDIM)
    scores = jnp.where(live, scores, -jnp.inf)
    top = jnp.max(scores, axis=1, keepdims=True)
    exponent = jnp.exp(scores - top)
    total = jnp.sum(exponent, axis=1, keepdims=True)
    return top, total, jnp.dot(exponent.astype(jnp.bfloat16), values, preferred_element_type=jnp.float32)


def head_columns(half, width):
    return slice(2 * half * width, (2 * half + 1) * width), slice((2 * half + 1) * width, (2 * half + 2) * width)


def layer_attend_first(
    tick, info_ref, q_ref, own_ref, other_ref, w_own_ref, w_other_ref, out_ref, kv_out, w_out_ref, sem_ref
):
    chips, halves, tokens, width = out_ref.shape
    slots, frames = kv_out.shape[:2]
    rows = frames * tokens
    slot = slot_of(info_ref, tick)
    core = lax.rem(info_ref[slots + 1], CORES)
    copies = side_by_side(core, width, w_own_ref, w_other_ref, w_out_ref, sem_ref, 0)
    for copy in copies:
        copy.start()
    both = 2 * width
    dims = (slots // CORES, frames, tokens, both)
    for mine in range(CORES):

        @pl.when(core == mine)
        def _():
            for half, ref in enumerate((own_ref, other_ref) if mine == 0 else (other_ref, own_ref)):
                for part in range(CORES):
                    kv_out[part * dims[0]:(part + 1) * dims[0], :, :, half * both:(half + 1) * both] = ref[
                        tokens:, part * both:(part + 1) * both
                    ].reshape(dims)

    kv_out[slot, core] = own_ref[:tokens]
    kv_out[slot, 1 - core] = other_ref[:tokens]
    _, live = live_keys(info_ref, slots, rows, tokens)
    for half in range(halves):
        key_columns, value_columns = head_columns(half, width)
        _, total, attended = softmax_part(
            q_ref[:, half * width:(half + 1) * width],
            kv_out[:, :, :, key_columns].reshape(slots * rows, width),
            kv_out[:, :, :, value_columns].reshape(slots * rows, width),
            live,
        )
        attended = (attended / total).astype(jnp.bfloat16)
        for chip in range(chips):
            out_ref[chip, half] = attended
    for copy in copies:
        copy.wait()


def layer_attend_most(tick, info_ref, xn_ref, w_ref, own_ref, kv_ref, *refs):
    *late_ref, q_ref, kv_out, acc_ref, top_ref, total_ref = refs
    slots, frames, tokens, _ = kv_out.shape
    rows = frames * tokens
    width = HDIM
    slot = slot_of(info_ref, tick)
    core = lax.rem(info_ref[slots + 1], CORES)
    q_ref[...] = jnp.dot(xn_ref[...], w_ref[...], preferred_element_type=jnp.float32).astype(jnp.bfloat16)
    kv_out[...] = kv_ref[...]
    for ref in late_ref:
        kv_out[slot_of(info_ref, tick - 1), 1 - core] = ref[...]
    kv_out[slot, core] = own_ref[...]
    key_ids, live = live_keys(info_ref, slots, rows, tokens)
    missing = slot * rows + (1 - core) * tokens
    live = live & ((key_ids < missing) | (key_ids >= missing + tokens))
    for half in range(acc_ref.shape[0]):
        key_columns, value_columns = head_columns(half, width)
        top, total, acc = softmax_part(
            q_ref[:, half * width:(half + 1) * width],
            kv_out[:, :, :, key_columns].reshape(slots * rows, width),
            kv_out[:, :, :, value_columns].reshape(slots * rows, width),
            live,
        )
        acc_ref[half] = acc
        top_ref[half] = jnp.broadcast_to(top, (tokens, width))
        total_ref[half] = jnp.broadcast_to(total, (tokens, width))


def layer_attend_rest(tick, info_ref, q_ref, other_ref, acc_ref, top_ref, total_ref, out_ref):
    chips, halves, tokens, width = out_ref.shape
    core = lax.rem(info_ref[info_ref.shape[0] - 1], CORES)
    live = 1 - core < info_ref[slot_of(info_ref, tick)]
    for half in range(halves):
        key_columns, value_columns = head_columns(half, width)
        scores = lax.dot_general(
            q_ref[:, half * width:(half + 1) * width], other_ref[:, key_columns], (((1,), (1,)), ((), ())),
            preferred_element_type=jnp.float32,
        ) / math.sqrt(HDIM)
        scores = jnp.where(live, scores, -jnp.inf)
        before = top_ref[half]
        top = jnp.maximum(before, jnp.max(scores, axis=1, keepdims=True))
        exponent = jnp.exp(scores - top[:, :1])
        shrink = jnp.exp(before - top)
        total = total_ref[half] * shrink + jnp.sum(exponent, axis=1, keepdims=True)
        attended = acc_ref[half] * shrink + jnp.dot(
            exponent.astype(jnp.bfloat16), other_ref[:, value_columns], preferred_element_type=jnp.float32
        )
        attended = (attended / total).astype(jnp.bfloat16)
        for chip in range(chips):
            out_ref[chip, half] = attended


def layer_back(tick, info_ref, a_ref, w_ref, x_ref, out_ref, wide_ref):
    chips, halves, tokens, width = a_ref.shape
    chip = lax.div(info_ref[info_ref.shape[0] - 1], CORES)
    live = core_live(info_ref, tick)
    for source in range(chips):
        for half in range(halves):
            first = (source * halves + half) * width
            wide_ref[:, first:first + width] = a_ref[source, half]
    branch = jnp.dot(wide_ref[...], w_ref[...], preferred_element_type=jnp.float32).astype(jnp.bfloat16)
    for half in range(halves):
        total = x_ref[chip, half].astype(jnp.float32) + branch[:, half * width:(half + 1) * width].astype(jnp.float32)
        out_ref[half] = jnp.where(live, total, 0.0).astype(jnp.bfloat16)


def pack_last(*refs):
    *result_refs, out_ref, wide_ref = refs
    group, parts, _ = out_ref.shape
    ticks = len(result_refs)
    for tick, ref in enumerate(result_refs):
        halves, tokens, _ = ref.shape
        for half in range(halves):
            first = (half * ticks + tick) * tokens
            wide_ref[first:first + tokens] = ref[half].astype(jnp.float32)
    for target in range(group):
        out_ref[target] = wide_ref[pl.ds(target, parts, stride=group), :].astype(jnp.bfloat16)


def unpack_last(info_ref, came_ref, out_ref, turn_ref):
    group, parts, width = came_ref.shape
    patches, frames, local, _ = out_ref.shape
    each = parts // CORES
    for source in range(group):
        chip, frame = divmod(source, CORES)
        wide = came_ref[source].astype(jnp.float32)
        for half in range(CORES):
            first = (chip * CORES + half) * width
            turn_ref[frame * each:(frame + 1) * each, first:first + width] = wide[half * each:(half + 1) * each]
    for tick in range(patches):
        slot = slot_of(info_ref, tick)
        for frame in range(frames):
            row = frame * each + tick * local
            out_ref[slot, frame] = turn_ref[row:row + local].astype(jnp.bfloat16)


def swap(value, groups=None):
    return lax.all_to_all(value, "seq", split_axis=0, concat_axis=0, tiled=True, axis_index_groups=groups)


def on_device(in_flight, entering, patch_frames, norm_gain, qkv_weight, out_weight, stale_kv):
    section = lax.axis_index("section")
    sections = lax.axis_size("section")
    me = lax.axis_index("seq")
    group = lax.axis_size("seq")
    patches, frames, tokens = stale_kv.shape[1:4]
    local = in_flight.shape[2]
    width = in_flight.shape[3]
    ticks = patches
    chips = group // CORES
    halves = CORES
    owned = local * group
    same_core = [[CORES * chip + core for chip in range(chips)] for core in range(CORES)]
    partner = [(device, device ^ 1) for device in range(group)]
    info = jnp.concatenate([patch_frames, jnp.stack([section, me]).astype(jnp.int32)])

    w_in = jnp.transpose(qkv_weight[0], (1, 0, 2))
    w_in_other = lax.ppermute(w_in, "seq", partner)
    sent = call(
        pack_first,
        "pack_first",
        shape(group, owned + SPARE, HDIM),
        (),
        (in_flight, entering),
        [
            pltpu.VMEM(in_flight.shape, jnp.bfloat16),
            pltpu.VMEM(entering.shape, jnp.bfloat16),
            pltpu.VMEM((frames * owned, HDIM), jnp.float32),
            pltpu.VMEM((group * SPARE, HDIM), jnp.float32),
            pltpu.SemaphoreType.DMA((2,)),
        ],
        in_hbm=(0, 1),
    )
    sent, w_out_own = lax.optimization_barrier((sent, out_weight[0]))
    came = swap(sent)
    w_out_other = lax.ppermute(w_out_own, "seq", partner)
    stale = stale_kv[0].reshape(patches * frames * tokens, 2 * HDIM)
    gathered, fresh, w_kv, w_q = call(
        functools.partial(unpack_first, local),
        "unpack_first",
        (
            shape(chips, halves, tokens, HDIM),
            shape(ticks - 1, halves, tokens, HDIM),
            kept(width, 2 * halves * HDIM),
            kept(width, halves * HDIM),
        ),
        (info,),
        (came, w_in, w_in_other),
        [
            pltpu.VMEM(came.shape, jnp.bfloat16),
            pltpu.VMEM((group * (owned + SPARE), HDIM), jnp.float32),
            pltpu.SemaphoreType.DMA((1,)),
            pltpu.SemaphoreType.DMA((3, CORES)),
        ],
        in_hbm=(1,),
        anywhere=(0, 2),
    )
    new_rows = tokens + patches * frames * tokens // CORES
    results = []
    for tick in range(ticks):
        if tick:
            arrived = lax.ppermute(
                results[-1], "section", [(source, source + 1) for source in range(sections - 1)]
            )
            arrived = jnp.where(section == 0, fresh[tick - 1], arrived)
            gathered = swap(jnp.broadcast_to(arrived[None], (chips,) + arrived.shape), same_core)
        normed, own = call(
            functools.partial(layer_keys, tick),
            "keys",
            (shape(tokens, width), shape(tokens if tick else new_rows, 2 * halves * HDIM)),
            (info,),
            (gathered, norm_gain, w_kv) + (() if tick else (stale,)),
        )
        other = lax.ppermute(own, "seq", partner)
        kv_dims = (patches, frames, tokens, 2 * halves * HDIM)
        sent_dims = (chips, halves, tokens, HDIM)
        if tick == 0:
            queries = call(layer_queries, "queries", shape(tokens, halves * HDIM), (), (normed, w_q))
            attended, kv, w_out = call(
                functools.partial(layer_attend_first, tick),
                "attend_first",
                (shape(*sent_dims), shape(*kv_dims), kept(width, halves * HDIM)),
                (info,),
                (queries, own, other, out_weight[0], w_out_other),
                [pltpu.SemaphoreType.DMA((CORES,))],
                in_hbm=(3,),
                anywhere=(4,),
            )
            late = ()
        else:
            per_head = jax.ShapeDtypeStruct((halves, tokens, HDIM), jnp.float32)
            queries, kv, *part = call(
                functools.partial(layer_attend_most, tick),
                "attend_most",
                (shape(tokens, halves * HDIM), shape(*kv_dims), per_head, per_head, per_head),
                (info,),
                (normed, w_q, own, kv) + late,
            )
            attended = call(
                functools.partial(layer_attend_rest, tick),
                "attend_rest",
                shape(*sent_dims),
                (info,),
                (queries, other, *part),
            )
            late = (other,)
        results.append(
            call(
                functools.partial(layer_back, tick),
                "back",
                shape(halves, tokens, HDIM),
                (info,),
                (swap(attended, same_core), w_out, gathered),
                [pltpu.VMEM((tokens, width), jnp.bfloat16)],
            )
        )

    parts = ticks * halves * local
    sent = call(
        pack_last,
        "pack_last",
        shape(group, parts, HDIM),
        (),
        tuple(results),
        [pltpu.VMEM((ticks * halves * tokens, HDIM), jnp.float32)],
    )
    outputs = call(
        unpack_last,
        "unpack_last",
        shape(patches, frames, local, width),
        (info,),
        (swap(sent),),
        [pltpu.VMEM((parts, width), jnp.float32)],
    )
    return outputs[None]


def solution(mesh):
    in_specs = (
        P("section", None, "seq", None),
        P(None, None, "seq", None),
        P(),
        P("section", None),
        P("section", None, None, "seq"),
        P("section", None, "seq"),
        P("section", None, None, None, None, "seq"),
    )
    out_specs = P("section", None, None, "seq", None)
    return jax.shard_map(
        on_device, mesh=mesh, in_specs=in_specs, out_specs=out_specs, check_vma=False
    )
```

```python
import functools
import math

import jax
import jax.numpy as jnp
from jax import lax
from jax.experimental import pallas as pl
from jax.experimental.pallas import tpu as pltpu
from jax.sharding import PartitionSpec as P

HDIM = 128
CORES = 2
WEIGHT_PARTS = 4
MOST_SECTIONS = 1024
SPARE = 16
VMEM_LIMIT = 12 * 1024 * 1024


def call(body, name, out_shape, scalars, arrays, scratch=(), in_hbm=(), anywhere=()):
    arrays = [
        pltpu.with_memory_space_constraint(array, pltpu.HBM) if place in in_hbm else array
        for place, array in enumerate(arrays)
    ]
    in_vmem = pl.BlockSpec(memory_space=pltpu.VMEM)
    in_smem = pl.BlockSpec(memory_space=pltpu.SMEM)
    return pl.pallas_call(
        body,
        out_shape=out_shape,
        in_specs=[in_smem] * len(scalars)
        + [pl.BlockSpec(memory_space=pl.ANY) if place in (*in_hbm, *anywhere) else in_vmem for place in range(len(arrays))],
        out_specs=jax.tree.map(lambda _: in_vmem, out_shape),
        scratch_shapes=list(scratch),
        compiler_params=pltpu.CompilerParams(vmem_limit_bytes=VMEM_LIMIT),
        name=name,
    )(*scalars, *arrays)


def shape(*dims):
    return jax.ShapeDtypeStruct(dims, jnp.bfloat16)


def pack_first(mine_any, later_any, ready_any, out_ref, mine_ref, later_ref, rows_ref, spare_ref, sem_ref):
    _, frames, local, width = mine_ref.shape
    copies = [
        pltpu.make_async_copy(mine_any, mine_ref, sem_ref.at[0]),
        pltpu.make_async_copy(later_any, later_ref, sem_ref.at[1]),
    ]
    for copy in copies:
        copy.start()
    spare_ref[...] = jnp.zeros_like(spare_ref)
    for copy in copies:
        copy.wait()
    group = out_ref.shape[0]
    blocks = width // HDIM
    each = local * blocks
    for frame in range(frames):
        wide = mine_ref[0, frame].astype(jnp.float32)
        for block in range(blocks):
            rows_ref[pl.ds(frame * each + block, local, stride=blocks), :] = wide[:, block * HDIM:(block + 1) * HDIM]
    for tick in range(later_ref.shape[0]):
        for frame in range(frames):
            wide = later_ref[tick, frame].astype(jnp.float32)
            for block in range(blocks):
                chip, half = divmod(block, CORES)
                row = (chip * CORES + frame) * SPARE + tick * local * CORES + half
                spare_ref[pl.ds(row, local, stride=CORES), :] = wide[:, block * HDIM:(block + 1) * HDIM]
    for target in range(group):
        frame = target % CORES
        out_ref[target, :each] = rows_ref[frame * each:(frame + 1) * each].astype(jnp.bfloat16)
        out_ref[target, each:] = spare_ref[target * SPARE:(target + 1) * SPARE].astype(jnp.bfloat16)


def side_by_side(core, wide, own_ref, other_ref, out_ref, sem_ref, first):
    copies = []
    for index, (ref, place) in enumerate(((own_ref, core), (other_ref, 1 - core))):
        columns = pl.ds(pl.multiple_of(place * wide + first, HDIM), HDIM)
        copies.append(pltpu.make_async_copy(ref, out_ref.at[:, columns], sem_ref.at[index]))
    return copies


def unpack_first(
    local, came_any, own_ref, other_ref, hidden_ref, fresh_ref, wkv_ref, wq_ref, came_ref, wide_ref, came_sem, sem_ref
):
    group, rows, _ = came_ref.shape
    chips, halves = hidden_ref.shape[:2]
    blocks = chips * halves
    core = own_core()
    first_copy = pltpu.make_async_copy(came_any, came_ref, came_sem.at[0])
    first_copy.start()
    copies = []
    for kind, (out_ref, wide, first) in enumerate(((wq_ref, HDIM, 0), (wkv_ref, 2 * HDIM, 0), (wkv_ref, 2 * HDIM, HDIM))):
        copies += side_by_side(core, wide, own_ref.at[kind], other_ref.at[kind], out_ref, sem_ref.at[kind], first)
    for copy in copies:
        copy.start()
    first_copy.wait()
    for source in range(group):
        wide_ref[source * rows:(source + 1) * rows] = came_ref[source].astype(jnp.float32)

    def over_sources(row):
        return wide_ref[pl.ds(row, group, stride=rows), :].astype(jnp.bfloat16)

    for t in range(local):
        for block in range(blocks):
            hidden_ref[block // halves, block % halves, t * group:(t + 1) * group] = over_sources(t * blocks + block)
    for tick in range(fresh_ref.shape[0]):
        for t in range(local):
            for half in range(halves):
                fresh_ref[tick, half, t * group:(t + 1) * group] = over_sources(
                    local * blocks + (tick * local + t) * halves + half
                )
    for copy in copies:
        copy.wait()


def slot_of(frames_ref, tick):
    slots = frames_ref.shape[0]
    return lax.rem(tick + slots * MOST_SECTIONS - lax.axis_index("section"), slots)


def own_core():
    return lax.rem(lax.axis_index("seq"), CORES)


def core_live(frames_ref, tick):
    return own_core() < frames_ref[slot_of(frames_ref, tick)]


def first_rows(tokens, slot_rows, width):
    stale = tokens + slot_rows // CORES
    return stale, stale + width // WEIGHT_PARTS


def layer_keys(tick, frames_ref, x_ref, gain_ref, w_ref, *refs):
    *first_refs, xn_ref, new_ref = refs if tick else refs[:-1]
    copies = []
    if tick == 0:
        stale_ref, out_any = first_refs
        sem_ref = refs[-1]
        stale_end, weight_end = first_rows(x_ref.shape[2], stale_ref.shape[0], out_any.shape[0])
        part_rows = weight_end - stale_end
        for part in range(WEIGHT_PARTS):
            copies.append(
                pltpu.make_async_copy(
                    out_any.at[part * part_rows:(part + 1) * part_rows],
                    new_ref.at[stale_end:weight_end, part * HDIM:(part + 1) * HDIM],
                    sem_ref.at[part],
                )
            )
            copies[-1].start()
    chips, halves, tokens, width = x_ref.shape
    squares = jnp.zeros((tokens, width), jnp.float32)
    for chip in range(chips):
        for half in range(halves):
            wide = x_ref[chip, half].astype(jnp.float32)
            squares = squares + wide * wide
    mean_square = jnp.sum(squares, axis=1, keepdims=True) / (chips * halves * width)
    scale = jnp.where(core_live(frames_ref, tick), lax.rsqrt(mean_square + 1e-06), 0.0)
    for chip in range(chips):
        for half in range(halves):
            first = (chip * halves + half) * width
            wide = x_ref[chip, half].astype(jnp.float32)
            normed = wide * scale * gain_ref[:, first:first + width].astype(jnp.float32)
            xn_ref[:, first:first + width] = normed.astype(jnp.bfloat16)
    new_ref[:tokens] = jnp.dot(xn_ref[...], w_ref[...], preferred_element_type=jnp.float32).astype(jnp.bfloat16)
    if tick == 0:
        rows, both = stale_ref.shape
        for part in range(CORES):
            new_ref[tokens:stale_end, part * both:(part + 1) * both] = stale_ref[
                part * rows // CORES:(part + 1) * rows // CORES
            ]
        for copy in copies:
            copy.wait()


def layer_queries(xn_ref, w_ref, out_ref):
    out_ref[...] = jnp.dot(xn_ref[...], w_ref[...], preferred_element_type=jnp.float32).astype(jnp.bfloat16)


def layer_attend(tick, frames_ref, q_ref, own_ref, other_ref, *refs):
    *kv_ref, out_ref, kv_out = refs if tick else refs[:2]
    chips, halves, tokens, width = out_ref.shape
    slots, frames = kv_out.shape[:2]
    rows = frames * tokens
    slot = slot_of(frames_ref, tick)
    core = own_core()
    for ref in kv_ref:
        kv_out[...] = ref[...]
    copies = []
    if tick == 0:
        w_out_ref, sem_ref = refs[2:]
        both = 2 * width
        stale_end, weight_end = first_rows(tokens, slots * rows, w_out_ref.shape[0])
        for part in range(WEIGHT_PARTS):
            source = (slice(stale_end, weight_end), slice(part * width, (part + 1) * width))
            target = w_out_ref.at[part * (weight_end - stale_end):(part + 1) * (weight_end - stale_end)]
            copies += side_by_side(core, width, own_ref.at[source], other_ref.at[source], target, sem_ref.at[part], 0)
        for copy in copies:
            copy.start()
        dims = (slots // CORES, frames, tokens, both)
        for mine in range(CORES):

            @pl.when(core == mine)
            def _():
                for half, ref in enumerate((own_ref, other_ref) if mine == 0 else (other_ref, own_ref)):
                    for part in range(CORES):
                        kv_out[part * dims[0]:(part + 1) * dims[0], :, :, half * both:(half + 1) * both] = ref[
                            tokens:stale_end, part * both:(part + 1) * both
                        ].reshape(dims)

    kv_out[slot, core] = own_ref[:tokens]
    kv_out[slot, 1 - core] = other_ref[:tokens]
    key_ids = lax.broadcasted_iota(jnp.int32, (1, slots * rows), 1)
    key_slot = key_ids // rows
    limit = jnp.zeros_like(key_ids)
    for patch in range(slots):
        limit = jnp.where(key_slot == patch, frames_ref[patch] * tokens, limit)
    key_live = key_ids - key_slot * rows < limit
    for half in range(halves):
        queries = q_ref[:, half * width:(half + 1) * width]
        keys = kv_out[:, :, :, 2 * half * width:(2 * half + 1) * width].reshape(slots * rows, width)
        values = kv_out[:, :, :, (2 * half + 1) * width:(2 * half + 2) * width].reshape(slots * rows, width)
        scores = lax.dot_general(
            queries, keys, (((1,), (1,)), ((), ())), preferred_element_type=jnp.float32
        ) / math.sqrt(HDIM)
        scores = jnp.where(key_live, scores, -jnp.inf)
        exponent = jnp.exp(scores - jnp.max(scores, axis=1, keepdims=True))
        row_total = jnp.sum(exponent, axis=1, keepdims=True)
        attended = jnp.dot(exponent.astype(jnp.bfloat16), values, preferred_element_type=jnp.float32)
        attended = (attended / row_total).astype(jnp.bfloat16)
        for chip in range(chips):
            out_ref[chip, half] = attended
    for copy in copies:
        copy.wait()


def spread(tick, fresh_ref, arrived_ref, out_ref):
    rows = jnp.where(lax.axis_index("section") == 0, fresh_ref[tick - 1], arrived_ref[...])
    for chip in range(out_ref.shape[0]):
        out_ref[chip] = rows


def layer_back(tick, frames_ref, a_ref, w_ref, x_ref, out_ref, wide_ref):
    chips, halves, tokens, width = a_ref.shape
    chip = lax.div(lax.axis_index("seq"), CORES)
    live = core_live(frames_ref, tick)
    for source in range(chips):
        for half in range(halves):
            first = (source * halves + half) * width
            wide_ref[:, first:first + width] = a_ref[source, half]
    branch = jnp.dot(wide_ref[...], w_ref[...], preferred_element_type=jnp.float32).astype(jnp.bfloat16)
    for half in range(halves):
        total = x_ref[chip, half].astype(jnp.float32) + branch[:, half * width:(half + 1) * width].astype(jnp.float32)
        out_ref[half] = jnp.where(live, total, 0.0).astype(jnp.bfloat16)


def pack_last(*refs):
    *result_refs, out_ref, wide_ref = refs
    group, parts, _ = out_ref.shape
    ticks = len(result_refs)
    for tick, ref in enumerate(result_refs):
        halves, tokens, _ = ref.shape
        for half in range(halves):
            first = (half * ticks + tick) * tokens
            wide_ref[first:first + tokens] = ref[half].astype(jnp.float32)
    for target in range(group):
        out_ref[target] = wide_ref[pl.ds(target, parts, stride=group), :].astype(jnp.bfloat16)


def unpack_last(frames_ref, came_ref, out_ref, turn_ref):
    group, parts, width = came_ref.shape
    patches, frames, local, _ = out_ref.shape
    each = parts // CORES
    for source in range(group):
        chip, frame = divmod(source, CORES)
        wide = came_ref[source].astype(jnp.float32)
        for half in range(CORES):
            first = (chip * CORES + half) * width
            turn_ref[frame * each:(frame + 1) * each, first:first + width] = wide[half * each:(half + 1) * each]
    for tick in range(patches):
        slot = slot_of(frames_ref, tick)
        for frame in range(frames):
            row = frame * each + tick * local
            out_ref[slot, frame] = turn_ref[row:row + local].astype(jnp.bfloat16)


def swap(value, groups=None):
    return lax.all_to_all(value, "seq", split_axis=0, concat_axis=0, tiled=True, axis_index_groups=groups)


def on_device(in_flight, entering, patch_frames, norm_gain, qkv_weight, out_weight, stale_kv):
    sections = lax.axis_size("section")
    group = lax.axis_size("seq")
    patches, frames, tokens = stale_kv.shape[1:4]
    local = in_flight.shape[2]
    width = in_flight.shape[3]
    ticks = patches
    chips = group // CORES
    halves = CORES
    owned = local * group
    same_core = [[CORES * chip + core for chip in range(chips)] for core in range(CORES)]
    partner = [(device, device ^ 1) for device in range(group)]

    w_in = jnp.transpose(qkv_weight[0], (1, 0, 2))
    w_in_other = lax.ppermute(w_in, "seq", partner)
    stale = stale_kv[0].reshape(patches * frames * tokens, 2 * HDIM)
    sent = call(
        pack_first,
        "pack_first",
        shape(group, owned + SPARE, HDIM),
        (),
        (in_flight, entering, stale),
        [
            pltpu.VMEM(in_flight.shape, jnp.bfloat16),
            pltpu.VMEM(entering.shape, jnp.bfloat16),
            pltpu.VMEM((frames * owned, HDIM), jnp.float32),
            pltpu.VMEM((group * SPARE, HDIM), jnp.float32),
            pltpu.SemaphoreType.DMA((2,)),
        ],
        in_hbm=(0, 1),
        anywhere=(2,),
    )
    came = swap(sent)
    gathered, fresh, w_kv, w_q = call(
        functools.partial(unpack_first, local),
        "unpack_first",
        (
            shape(chips, halves, tokens, HDIM),
            shape(ticks - 1, halves, tokens, HDIM),
            shape(width, 2 * halves * HDIM),
            shape(width, halves * HDIM),
        ),
        (),
        (came, w_in, w_in_other),
        [
            pltpu.VMEM(came.shape, jnp.bfloat16),
            pltpu.VMEM((group * (owned + SPARE), HDIM), jnp.float32),
            pltpu.SemaphoreType.DMA((1,)),
            pltpu.SemaphoreType.DMA((3, CORES)),
        ],
        in_hbm=(1,),
        anywhere=(0, 2),
    )
    results = []
    for tick in range(ticks):
        if tick:
            arrived = lax.ppermute(
                results[-1], "section", [(source, source + 1) for source in range(sections - 1)]
            )
            gathered = call(
                functools.partial(spread, tick), "spread", shape(chips, halves, tokens, HDIM), (), (fresh, arrived)
            )
            gathered = swap(gathered, same_core)
        new_rows = tokens if tick else first_rows(tokens, stale.shape[0], width)[1]
        normed, own = call(
            functools.partial(layer_keys, tick),
            "keys",
            (shape(tokens, width), shape(new_rows, 2 * halves * HDIM)),
            (patch_frames,),
            (gathered, norm_gain, w_kv) + (() if tick else (stale, out_weight[0])),
            () if tick else [pltpu.SemaphoreType.DMA((WEIGHT_PARTS,))],
            in_hbm=() if tick else (4,),
        )
        other = lax.ppermute(own, "seq", partner)
        queries = call(layer_queries, "queries", shape(tokens, halves * HDIM), (), (normed, w_q))
        attended, kv, *joined = call(
            functools.partial(layer_attend, tick),
            "attend",
            (shape(chips, halves, tokens, HDIM), shape(patches, frames, tokens, 2 * halves * HDIM))
            + (() if tick else (shape(width, halves * HDIM),)),
            (patch_frames,),
            (queries, own, other) + ((kv,) if tick else ()),
            () if tick else [pltpu.SemaphoreType.DMA((WEIGHT_PARTS, CORES))],
        )
        if tick == 0:
            (w_out,) = joined
        results.append(
            call(
                functools.partial(layer_back, tick),
                "back",
                shape(halves, tokens, HDIM),
                (patch_frames,),
                (swap(attended, same_core), w_out, gathered),
                [pltpu.VMEM((tokens, width), jnp.bfloat16)],
            )
        )

    parts = ticks * halves * local
    sent = call(
        pack_last,
        "pack_last",
        shape(group, parts, HDIM),
        (),
        tuple(results),
        [pltpu.VMEM((ticks * halves * tokens, HDIM), jnp.float32)],
    )
    outputs = call(
        unpack_last,
        "unpack_last",
        shape(patches, frames, local, width),
        (patch_frames,),
        (swap(sent),),
        [pltpu.VMEM((parts, width), jnp.float32)],
    )
    return outputs[None]


def solution(mesh):
    in_specs = (
        P("section", None, "seq", None),
        P(None, None, "seq", None),
        P(),
        P("section", None),
        P("section", None, None, "seq"),
        P("section", None, "seq"),
        P("section", None, None, None, None, "seq"),
    )
    out_specs = P("section", None, None, "seq", None)
    return jax.shard_map(
        on_device, mesh=mesh, in_specs=in_specs, out_specs=out_specs, check_vma=False
    )
```

```python
import functools
import math

import jax
import jax.numpy as jnp
from jax import lax
from jax.experimental import pallas as pl
from jax.experimental.pallas import tpu as pltpu
from jax.sharding import PartitionSpec as P

HDIM = 128
CORES = 2
WEIGHT_PARTS = 4
MOST_SECTIONS = 1024
SPARE = 32
VMEM_LIMIT = 12 * 1024 * 1024


def call(body, name, out_shape, scalars, arrays, scratch=(), in_hbm=(), anywhere=(), aliases=()):
    arrays = [
        pltpu.with_memory_space_constraint(array, pltpu.HBM) if place in in_hbm else array
        for place, array in enumerate(arrays)
    ]
    in_vmem = pl.BlockSpec(memory_space=pltpu.VMEM)
    in_smem = pl.BlockSpec(memory_space=pltpu.SMEM)
    return pl.pallas_call(
        body,
        out_shape=out_shape,
        in_specs=[in_smem] * len(scalars)
        + [pl.BlockSpec(memory_space=pl.ANY) if place in (*in_hbm, *anywhere) else in_vmem for place in range(len(arrays))],
        out_specs=jax.tree.map(lambda _: in_vmem, out_shape),
        scratch_shapes=list(scratch),
        input_output_aliases=dict(aliases),
        compiler_params=pltpu.CompilerParams(vmem_limit_bytes=VMEM_LIMIT),
        name=name,
    )(*scalars, *arrays)


def shape(*dims):
    return jax.ShapeDtypeStruct(dims, jnp.bfloat16)


def pack_first(mine_any, later_any, ready_any, out_ref, mine_ref, later_ref, rows_ref, spare_ref, sem_ref):
    _, frames, local, width = mine_ref.shape
    copies = [
        pltpu.make_async_copy(mine_any, mine_ref, sem_ref.at[0]),
        pltpu.make_async_copy(later_any, later_ref, sem_ref.at[1]),
    ]
    for copy in copies:
        copy.start()
    spare_ref[...] = jnp.zeros_like(spare_ref)
    for copy in copies:
        copy.wait()
    chips = out_ref.shape[0]
    blocks = width // HDIM
    each = local * blocks
    for frame in range(frames):
        wide = mine_ref[0, frame].astype(jnp.float32)
        for block in range(blocks):
            rows_ref[pl.ds(frame * each + block, local, stride=blocks), :] = wide[:, block * HDIM:(block + 1) * HDIM]
    for tick in range(later_ref.shape[0]):
        for frame in range(frames):
            wide = later_ref[tick, frame].astype(jnp.float32)
            for block in range(blocks):
                chip, half = divmod(block, CORES)
                row = chip * SPARE + (tick * frames + frame) * local * CORES + half
                spare_ref[pl.ds(row, local, stride=CORES), :] = wide[:, block * HDIM:(block + 1) * HDIM]
    rows = rows_ref[...].astype(jnp.bfloat16)
    for chip in range(chips):
        out_ref[chip, :frames * each] = rows
        out_ref[chip, frames * each:] = spare_ref[chip * SPARE:(chip + 1) * SPARE].astype(jnp.bfloat16)


def unpack_first(came_ref, weight_any, hidden_ref, fresh_ref, weight_ref, wide_ref, sem_ref):
    fetch = pltpu.make_async_copy(weight_any, weight_ref, sem_ref.at[0])
    fetch.start()
    chips, rows, _ = came_ref.shape
    halves, tokens = hidden_ref.shape[1:3]
    owned = tokens // chips
    blocks = chips * halves
    for source in range(chips):
        wide_ref[source * rows:(source + 1) * rows] = came_ref[source].astype(jnp.float32)

    def over_sources(row):
        return wide_ref[pl.ds(row, chips, stride=rows), :].astype(jnp.bfloat16)

    for token in range(owned):
        span = slice(token * chips, (token + 1) * chips)
        for block in range(blocks):
            hidden_ref[block // halves, block % halves, span] = over_sources(token * blocks + block)
        for tick in range(fresh_ref.shape[0]):
            for half in range(halves):
                fresh_ref[tick, half, span] = over_sources(
                    owned * blocks + (tick * owned + token) * halves + half
                )
    fetch.wait()


def slot_of(frames_ref, tick):
    slots = frames_ref.shape[0]
    return lax.rem(tick + slots * MOST_SECTIONS - lax.axis_index("section"), slots)


def own_core():
    return lax.rem(lax.axis_index("seq"), CORES)


def live_rows(frames, frames_ref, tick, rows):
    row_ids = lax.broadcasted_iota(jnp.int32, (rows, 1), 0)
    return row_ids < frames_ref[slot_of(frames_ref, tick)] * (rows // frames)


def first_rows(tokens, slot_rows, width):
    stale = tokens + slot_rows // CORES
    return stale, stale + width // WEIGHT_PARTS


def two_heads(own_ref, other_ref, kinds, span):
    return jnp.concatenate([ref[kind, span] for ref in (own_ref, other_ref) for kind in kinds], axis=1)


def layer_keys(tick, frames, frames_ref, x_ref, gain_ref, w_own_ref, w_other_ref, *refs):
    *first_refs, xn_ref, new_ref = refs
    chips, halves, tokens, width = x_ref.shape
    pair = halves * width
    squares = jnp.zeros((tokens, width), jnp.float32)
    for chip in range(chips):
        for half in range(halves):
            wide = x_ref[chip, half].astype(jnp.float32)
            squares = squares + wide * wide
    mean_square = jnp.sum(squares, axis=1, keepdims=True) / (chips * pair)
    scale = jnp.where(live_rows(frames, frames_ref, tick, tokens), lax.rsqrt(mean_square + 1e-06), 0.0)
    total = jnp.zeros((tokens, 2 * pair), jnp.float32)
    for chip in range(chips):
        span = slice(chip * pair, (chip + 1) * pair)
        wide = jnp.concatenate([x_ref[chip, half] for half in range(halves)], axis=1).astype(jnp.float32)
        normed = (wide * scale * gain_ref[:, span].astype(jnp.float32)).astype(jnp.bfloat16)
        xn_ref[:, span] = normed
        total = total + jnp.dot(
            normed, two_heads(w_own_ref, w_other_ref, (1, 2), span), preferred_element_type=jnp.float32
        )
    new_ref[:tokens] = total.astype(jnp.bfloat16)
    if tick == 0:
        stale_ref, out_ref = first_refs
        rows, both = stale_ref.shape
        stale_end, weight_end = first_rows(tokens, rows, out_ref.shape[0])
        for part in range(CORES):
            new_ref[tokens:stale_end, part * both:(part + 1) * both] = stale_ref[
                part * rows // CORES:(part + 1) * rows // CORES
            ]
        part_rows = weight_end - stale_end
        for part in range(WEIGHT_PARTS):
            new_ref[stale_end:weight_end, part * width:(part + 1) * width] = out_ref[
                part * part_rows:(part + 1) * part_rows
            ]


def layer_queries(xn_ref, w_own_ref, w_other_ref, out_ref):
    pair = out_ref.shape[1]
    total = jnp.zeros(out_ref.shape, jnp.float32)
    for first in range(0, xn_ref.shape[1], pair):
        span = slice(first, first + pair)
        total = total + jnp.dot(
            xn_ref[:, span], two_heads(w_own_ref, w_other_ref, (0,), span), preferred_element_type=jnp.float32
        )
    out_ref[...] = total.astype(jnp.bfloat16)


def layer_attend(tick, frames, frames_ref, q_ref, own_ref, other_ref, *refs):
    out_ref, kv_out = refs[-2:]
    chips, halves, tokens, width = out_ref.shape
    slots = kv_out.shape[0]
    rows = CORES * tokens
    span = tokens // frames
    both = 2 * width
    slot = slot_of(frames_ref, tick)
    core = own_core()
    if tick == 0:
        for place_of, ref in enumerate((own_ref, other_ref)):
            columns = slice(place_of * both, (place_of + 1) * both)
            for old in range(slots):
                part, place = divmod(old, slots // CORES)
                for frame in range(frames):
                    for piece in range(CORES):
                        row = tokens + place * rows + (frame * CORES + piece) * span
                        kv_out[old, piece, frame * span:(frame + 1) * span, columns] = ref[
                            row:row + span, part * both:(part + 1) * both
                        ]
    kv_out[slot, core] = own_ref[:tokens]
    kv_out[slot, 1 - core, :, :both] = other_ref[:tokens, both:]
    kv_out[slot, 1 - core, :, both:] = other_ref[:tokens, :both]
    key_ids = lax.broadcasted_iota(jnp.int32, (1, slots * rows), 1)
    limit = jnp.zeros_like(key_ids)
    for patch in range(slots):
        limit = jnp.where(key_ids // rows == patch, frames_ref[patch] * span, limit)
    key_live = key_ids % tokens < limit
    for head, half in enumerate((core, 1 - core)):
        queries = q_ref[:, head * width:(head + 1) * width]
        first = head * both
        keys = kv_out[:, :, :, first:first + width].reshape(slots * rows, width)
        values = kv_out[:, :, :, first + width:first + both].reshape(slots * rows, width)
        scores = lax.dot_general(
            queries, keys, (((1,), (1,)), ((), ())), preferred_element_type=jnp.float32
        ) * (1.0 / math.sqrt(HDIM))
        scores = jnp.where(key_live, scores, -jnp.inf)
        exponent = jnp.exp(scores - jnp.max(scores, axis=1, keepdims=True))
        row_total = jnp.sum(exponent, axis=1, keepdims=True)
        attended = jnp.dot(exponent.astype(jnp.bfloat16), values, preferred_element_type=jnp.float32)
        attended = (attended / row_total).astype(jnp.bfloat16)
        for chip in range(chips):
            out_ref[chip, half] = attended


def spread(tick, fresh_ref, arrived_ref, out_ref):
    rows = jnp.where(lax.axis_index("section") == 0, fresh_ref[tick - 1], arrived_ref[...])
    for chip in range(out_ref.shape[0]):
        out_ref[chip] = rows


def layer_back(tick, frames, slot_rows, frames_ref, a_ref, w_own_ref, first_other_ref, x_ref, out_ref):
    chips, halves, tokens, width = a_ref.shape
    pair = halves * width
    chip = lax.div(lax.axis_index("seq"), CORES)
    core = own_core()
    live = live_rows(frames, frames_ref, tick, tokens)
    stale_end, weight_end = first_rows(tokens, slot_rows, w_own_ref.shape[0])
    branch = jnp.zeros((tokens, pair), jnp.float32)
    for source in range(chips):
        wide = jnp.concatenate([a_ref[source, half] for half in range(halves)], axis=1)
        part, row = divmod(source * pair, weight_end - stale_end)
        row += stale_end
        weights = jnp.concatenate(
            [
                w_own_ref[source * pair:(source + 1) * pair],
                first_other_ref[row:row + pair, part * width:(part + 1) * width],
            ],
            axis=1,
        )
        branch = branch + jnp.dot(wide, weights, preferred_element_type=jnp.float32)
    branch = branch.astype(jnp.bfloat16).astype(jnp.float32)
    for head, half in enumerate((core, 1 - core)):
        total = x_ref[chip, half].astype(jnp.float32) + branch[:, head * width:(head + 1) * width]
        out_ref[half] = jnp.where(live, total, 0.0).astype(jnp.bfloat16)


def pack_last(*refs):
    *result_refs, out_ref, wide_ref = refs
    chips, parts, _ = out_ref.shape
    ticks = len(result_refs)
    for tick, ref in enumerate(result_refs):
        halves, tokens, _ = ref.shape
        for half in range(halves):
            first = (half * ticks + tick) * tokens
            wide_ref[first:first + tokens] = ref[half].astype(jnp.float32)
    for chip in range(chips):
        out_ref[chip] = wide_ref[pl.ds(chip, parts, stride=chips), :].astype(jnp.bfloat16)


def unpack_last(frames_ref, came_ref, out_ref, turn_ref):
    chips, parts, width = came_ref.shape
    patches, frames, local, _ = out_ref.shape
    each = parts // CORES
    for chip in range(chips):
        wide = came_ref[chip].astype(jnp.float32)
        for half in range(CORES):
            first = (chip * CORES + half) * width
            turn_ref[:, first:first + width] = wide[half * each:(half + 1) * each]
    for tick in range(patches):
        slot = slot_of(frames_ref, tick)
        for frame in range(frames):
            row = (tick * frames + frame) * local
            out_ref[slot, frame] = turn_ref[row:row + local].astype(jnp.bfloat16)


def on_device(in_flight, entering, patch_frames, norm_gain, qkv_weight, out_weight, stale_kv):
    sections = lax.axis_size("section")
    group = lax.axis_size("seq")
    patches, frames, tokens = stale_kv.shape[1:4]
    local = in_flight.shape[2]
    width = in_flight.shape[3]
    ticks = patches
    chips = group // CORES
    halves = CORES
    owned = frames * local
    rows = owned * chips
    blocks = chips * halves
    same_core = [[CORES * chip + core for chip in range(chips)] for core in range(CORES)]
    partner = [(device, device ^ 1) for device in range(group)]

    def swap(value):
        return lax.all_to_all(
            value, "seq", split_axis=0, concat_axis=0, tiled=True, axis_index_groups=same_core
        )

    w_in = jnp.transpose(qkv_weight[0], (1, 0, 2))
    w_in_other = lax.ppermute(w_in, "seq", partner)
    stale = stale_kv[0].reshape(patches * frames * tokens, 2 * HDIM)
    sent = call(
        pack_first,
        "pack_first",
        shape(chips, owned * blocks + SPARE, HDIM),
        (),
        (in_flight, entering, stale),
        [
            pltpu.VMEM(in_flight.shape, jnp.bfloat16),
            pltpu.VMEM(entering.shape, jnp.bfloat16),
            pltpu.VMEM((owned * blocks, HDIM), jnp.float32),
            pltpu.VMEM((chips * SPARE, HDIM), jnp.float32),
            pltpu.SemaphoreType.DMA((2,)),
        ],
        in_hbm=(0, 1),
        anywhere=(2,),
    )
    came = swap(sent)
    gathered, fresh, w_out = call(
        unpack_first,
        "unpack_first",
        (shape(chips, halves, rows, HDIM), shape(ticks - 1, halves, rows, HDIM), shape(width, HDIM)),
        (),
        (came, out_weight[0]),
        [pltpu.VMEM((chips * (owned * blocks + SPARE), HDIM), jnp.float32), pltpu.SemaphoreType.DMA((1,))],
        in_hbm=(1,),
    )
    results = []
    for tick in range(ticks):
        if tick:
            arrived = lax.ppermute(
                results[-1], "section", [(source, source + 1) for source in range(sections - 1)]
            )
            gathered = call(
                functools.partial(spread, tick), "spread", shape(chips, halves, rows, HDIM), (), (fresh, arrived)
            )
            gathered = swap(gathered)
        new_rows = rows if tick else first_rows(rows, stale.shape[0], width)[1]
        normed, own = call(
            functools.partial(layer_keys, tick, frames),
            "keys",
            (shape(rows, width), shape(new_rows, 2 * halves * HDIM)),
            (patch_frames,),
            (gathered, norm_gain, w_in, w_in_other) + (() if tick else (stale, w_out)),
        )
        other = lax.ppermute(own, "seq", partner)
        queries = call(layer_queries, "queries", shape(rows, halves * HDIM), (), (normed, w_in, w_in_other))
        attended, kv = call(
            functools.partial(layer_attend, tick, frames),
            "attend",
            (shape(chips, halves, rows, HDIM), shape(patches, CORES, rows, 2 * halves * HDIM)),
            (patch_frames,),
            (queries, own, other) + ((kv,) if tick else ()),
            aliases={4: 1} if tick else {},
        )
        if tick == 0:
            first_other = other
        results.append(
            call(
                functools.partial(layer_back, tick, frames, stale.shape[0]),
                "back",
                shape(halves, rows, HDIM),
                (patch_frames,),
                (swap(attended), w_out, first_other, gathered),
            )
        )

    parts = ticks * halves * owned
    sent = call(
        pack_last,
        "pack_last",
        shape(chips, parts, HDIM),
        (),
        tuple(results),
        [pltpu.VMEM((ticks * halves * rows, HDIM), jnp.float32)],
    )
    outputs = call(
        unpack_last,
        "unpack_last",
        shape(patches, frames, local, width),
        (patch_frames,),
        (swap(sent),),
        [pltpu.VMEM((ticks * owned, width), jnp.float32)],
    )
    return outputs[None]


def solution(mesh):
    in_specs = (
        P("section", None, "seq", None),
        P(None, None, "seq", None),
        P(),
        P("section", None),
        P("section", None, None, "seq"),
        P("section", None, "seq"),
        P("section", None, None, None, None, "seq"),
    )
    out_specs = P("section", None, None, "seq", None)
    return jax.shard_map(
        on_device, mesh=mesh, in_specs=in_specs, out_specs=out_specs, check_vma=False
    )
```

```python
import functools
import math

import jax
import jax.numpy as jnp
from jax import lax
from jax.experimental import pallas as pl
from jax.experimental.pallas import tpu as pltpu
from jax.sharding import PartitionSpec as P

HDIM = 128
CORES = 2
WEIGHT_PARTS = 4
MOST_SECTIONS = 1024
VMEM_LIMIT = 12 * 1024 * 1024


def call(body, name, out_shape, scalars, arrays, scratch=(), in_hbm=(), aliases=()):
    arrays = [
        pltpu.with_memory_space_constraint(array, pltpu.HBM) if place in in_hbm else array
        for place, array in enumerate(arrays)
    ]
    in_vmem = pl.BlockSpec(memory_space=pltpu.VMEM)
    in_smem = pl.BlockSpec(memory_space=pltpu.SMEM)
    return pl.pallas_call(
        body,
        out_shape=out_shape,
        in_specs=[in_smem] * len(scalars)
        + [pl.BlockSpec(memory_space=pl.ANY) if place in in_hbm else in_vmem for place in range(len(arrays))],
        out_specs=jax.tree.map(lambda _: in_vmem, out_shape),
        scratch_shapes=list(scratch),
        input_output_aliases=dict(aliases),
        compiler_params=pltpu.CompilerParams(vmem_limit_bytes=VMEM_LIMIT),
        name=name,
    )(*scalars, *arrays)


def shape(*dims):
    return jax.ShapeDtypeStruct(dims, jnp.bfloat16)


def fetch_rows(tokens_any, tokens_ref, rows_ref, sem_ref):
    fetch = pltpu.make_async_copy(tokens_any, tokens_ref, sem_ref.at[0])
    fetch.start()
    fetch.wait()
    frames, local, width = tokens_ref.shape
    blocks = width // HDIM
    for frame in range(frames):
        wide = tokens_ref[frame].astype(jnp.float32)
        for block in range(blocks):
            rows_ref[pl.ds(frame * local * blocks + block, local, stride=blocks), :] = wide[
                :, block * HDIM:(block + 1) * HDIM
            ]


def send_rows(rows_ref, out_ref):
    chips, halves, tokens, _ = out_ref.shape
    for half in range(halves):
        rows = rows_ref[half * tokens:(half + 1) * tokens].astype(jnp.bfloat16)
        for chip in range(chips):
            out_ref[chip, half] = rows


def pack_first(mine_any, out_ref, mine_ref, rows_ref, sem_ref):
    fetch_rows(mine_any.at[0], mine_ref, rows_ref, sem_ref)
    send_rows(rows_ref, out_ref)


def to_blocks(came_ref, hidden_ref, wide_ref):
    chips, halves, tokens, _ = came_ref.shape
    blocks = chips * halves
    for chip in range(chips):
        for half in range(halves):
            first = (chip * halves + half) * tokens
            wide_ref[first:first + tokens] = came_ref[chip, half].astype(jnp.float32)
    for token in range(tokens // chips):
        for block in range(blocks):
            hidden_ref[block // halves, block % halves, token * chips:(token + 1) * chips] = wide_ref[
                pl.ds(token * blocks + block, chips, stride=halves * tokens), :
            ].astype(jnp.bfloat16)


def unpack_first(came_ref, weight_any, stale_any, hidden_ref, weight_ref, stale_ref, wide_ref, sem_ref):
    fetches = [
        pltpu.make_async_copy(weight_any, weight_ref, sem_ref.at[0]),
        pltpu.make_async_copy(stale_any, stale_ref, sem_ref.at[1]),
    ]
    for fetch in fetches:
        fetch.start()
    to_blocks(came_ref, hidden_ref, wide_ref)
    for fetch in fetches:
        fetch.wait()


def spread(tick, entering_any, arrived_ref, out_ref, tokens_ref, rows_ref, sem_ref):
    section = lax.axis_index("section")

    @pl.when(section == 0)
    def _():
        fetch_rows(entering_any.at[tick - 1], tokens_ref, rows_ref, sem_ref)
        send_rows(rows_ref, out_ref)

    @pl.when(section != 0)
    def _():
        for chip in range(out_ref.shape[0]):
            out_ref[chip] = arrived_ref[...]


def arrange(came_ref, hidden_ref, wide_ref):
    @pl.when(lax.axis_index("section") == 0)
    def _():
        to_blocks(came_ref, hidden_ref, wide_ref)


def slot_of(frames_ref, tick):
    slots = frames_ref.shape[0]
    return lax.rem(tick + slots * MOST_SECTIONS - lax.axis_index("section"), slots)


def own_core():
    return lax.rem(lax.axis_index("seq"), CORES)


def live_rows(frames, frames_ref, tick, rows):
    row_ids = lax.broadcasted_iota(jnp.int32, (rows, 1), 0)
    return row_ids < frames_ref[slot_of(frames_ref, tick)] * (rows // frames)


def first_rows(tokens, slot_rows, width):
    stale = tokens + slot_rows // CORES
    return stale, stale + width // WEIGHT_PARTS


def two_heads(own_ref, other_ref, kinds, span):
    return jnp.concatenate([ref[kind, span] for ref in (own_ref, other_ref) for kind in kinds], axis=1)


def layer_keys(tick, frames, frames_ref, x_ref, gain_ref, w_own_ref, w_other_ref, *refs):
    *first_refs, xn_ref, new_ref = refs if tick else refs[:-1]
    chips, halves, tokens, width = x_ref.shape
    pair = halves * width
    squares = jnp.zeros((tokens, width), jnp.float32)
    for chip in range(chips):
        for half in range(halves):
            wide = x_ref[chip, half].astype(jnp.float32)
            squares = squares + wide * wide
    mean_square = jnp.sum(squares, axis=1, keepdims=True) / (chips * pair)
    scale = jnp.where(live_rows(frames, frames_ref, tick, tokens), lax.rsqrt(mean_square + 1e-06), 0.0)
    total = jnp.zeros((tokens, 2 * pair), jnp.float32)
    for chip in range(chips):
        span = slice(chip * pair, (chip + 1) * pair)
        wide = jnp.concatenate([x_ref[chip, half] for half in range(halves)], axis=1).astype(jnp.float32)
        normed = (wide * scale * gain_ref[:, span].astype(jnp.float32)).astype(jnp.bfloat16)
        xn_ref[:, span] = normed
        total = total + jnp.dot(
            normed, two_heads(w_own_ref, w_other_ref, (1, 2), span), preferred_element_type=jnp.float32
        )
    new_ref[:tokens] = total.astype(jnp.bfloat16)
    if tick == 0:
        stale_ref, out_ref = first_refs
        wide_ref = refs[-1]
        rows = stale_ref.shape[0] // 2
        stale_end, weight_end = first_rows(tokens, rows, out_ref.shape[0])
        wide_ref[...] = stale_ref[...].astype(jnp.float32)
        each = rows // CORES
        for part in range(CORES):
            for kind in range(2):
                first = (part * 2 + kind) * width
                new_ref[tokens:stale_end, first:first + width] = wide_ref[
                    pl.ds(part * 2 * each + kind, each, stride=2), :
                ].astype(jnp.bfloat16)
        part_rows = weight_end - stale_end
        for part in range(WEIGHT_PARTS):
            new_ref[stale_end:weight_end, part * width:(part + 1) * width] = out_ref[
                part * part_rows:(part + 1) * part_rows
            ]


def layer_queries(xn_ref, w_own_ref, w_other_ref, out_ref):
    pair = out_ref.shape[1]
    total = jnp.zeros(out_ref.shape, jnp.float32)
    for first in range(0, xn_ref.shape[1], pair):
        span = slice(first, first + pair)
        total = total + jnp.dot(
            xn_ref[:, span], two_heads(w_own_ref, w_other_ref, (0,), span), preferred_element_type=jnp.float32
        )
    out_ref[...] = total.astype(jnp.bfloat16)


def layer_attend(tick, frames, frames_ref, q_ref, own_ref, other_ref, *refs):
    out_ref, kv_out = refs[-2:]
    chips, halves, tokens, width = out_ref.shape
    slots = kv_out.shape[0]
    rows = CORES * tokens
    span = tokens // frames
    both = 2 * width
    slot = slot_of(frames_ref, tick)
    core = own_core()
    if tick == 0:
        for place_of, ref in enumerate((own_ref, other_ref)):
            columns = slice(place_of * both, (place_of + 1) * both)
            for old in range(slots):
                part, place = divmod(old, slots // CORES)
                for frame in range(frames):
                    for piece in range(CORES):
                        row = tokens + place * rows + (frame * CORES + piece) * span
                        kv_out[old, piece, frame * span:(frame + 1) * span, columns] = ref[
                            row:row + span, part * both:(part + 1) * both
                        ]
    kv_out[slot, core] = own_ref[:tokens]
    kv_out[slot, 1 - core, :, :both] = other_ref[:tokens, both:]
    kv_out[slot, 1 - core, :, both:] = other_ref[:tokens, :both]
    key_ids = lax.broadcasted_iota(jnp.int32, (1, slots * rows), 1)
    limit = jnp.zeros_like(key_ids)
    for patch in range(slots):
        limit = jnp.where(key_ids // rows == patch, frames_ref[patch] * span, limit)
    key_live = key_ids % tokens < limit
    for head, half in enumerate((core, 1 - core)):
        queries = q_ref[:, head * width:(head + 1) * width]
        first = head * both
        keys = kv_out[:, :, :, first:first + width].reshape(slots * rows, width)
        values = kv_out[:, :, :, first + width:first + both].reshape(slots * rows, width)
        scores = lax.dot_general(
            queries, keys, (((1,), (1,)), ((), ())), preferred_element_type=jnp.float32
        ) * (1.0 / math.sqrt(HDIM))
        scores = jnp.where(key_live, scores, -jnp.inf)
        exponent = jnp.exp(scores - jnp.max(scores, axis=1, keepdims=True))
        row_total = jnp.sum(exponent, axis=1, keepdims=True)
        attended = jnp.dot(exponent.astype(jnp.bfloat16), values, preferred_element_type=jnp.float32)
        attended = (attended / row_total).astype(jnp.bfloat16)
        for chip in range(chips):
            out_ref[chip, half] = attended


def layer_back(tick, frames, slot_rows, frames_ref, a_ref, w_own_ref, first_other_ref, x_ref, out_ref):
    chips, halves, tokens, width = a_ref.shape
    pair = halves * width
    chip = lax.div(lax.axis_index("seq"), CORES)
    core = own_core()
    live = live_rows(frames, frames_ref, tick, tokens)
    stale_end, weight_end = first_rows(tokens, slot_rows, w_own_ref.shape[0])
    branch = jnp.zeros((tokens, pair), jnp.float32)
    for source in range(chips):
        wide = jnp.concatenate([a_ref[source, half] for half in range(halves)], axis=1)
        part, row = divmod(source * pair, weight_end - stale_end)
        row += stale_end
        weights = jnp.concatenate(
            [
                w_own_ref[source * pair:(source + 1) * pair],
                first_other_ref[row:row + pair, part * width:(part + 1) * width],
            ],
            axis=1,
        )
        branch = branch + jnp.dot(wide, weights, preferred_element_type=jnp.float32)
    branch = branch.astype(jnp.bfloat16).astype(jnp.float32)
    for head, half in enumerate((core, 1 - core)):
        total = x_ref[chip, half].astype(jnp.float32) + branch[:, head * width:(head + 1) * width]
        out_ref[half] = jnp.where(live, total, 0.0).astype(jnp.bfloat16)


def pack_last(*refs):
    *result_refs, out_ref, wide_ref = refs
    chips, parts, _ = out_ref.shape
    ticks = len(result_refs)
    for tick, ref in enumerate(result_refs):
        halves, tokens, _ = ref.shape
        for half in range(halves):
            first = (half * ticks + tick) * tokens
            wide_ref[first:first + tokens] = ref[half].astype(jnp.float32)
    for chip in range(chips):
        out_ref[chip] = wide_ref[pl.ds(chip, parts, stride=chips), :].astype(jnp.bfloat16)


def unpack_last(frames_ref, came_ref, out_ref, turn_ref):
    chips, parts, width = came_ref.shape
    patches, frames, local, _ = out_ref.shape
    each = parts // CORES
    for chip in range(chips):
        wide = came_ref[chip].astype(jnp.float32)
        for half in range(CORES):
            first = (chip * CORES + half) * width
            turn_ref[:, first:first + width] = wide[half * each:(half + 1) * each]
    for tick in range(patches):
        slot = slot_of(frames_ref, tick)
        for frame in range(frames):
            row = (tick * frames + frame) * local
            out_ref[slot, frame] = turn_ref[row:row + local].astype(jnp.bfloat16)


def on_device(in_flight, entering, patch_frames, norm_gain, qkv_weight, out_weight, stale_kv):
    sections = lax.axis_size("section")
    group = lax.axis_size("seq")
    patches, frames, tokens = stale_kv.shape[1:4]
    local = in_flight.shape[2]
    width = in_flight.shape[3]
    ticks = patches
    chips = group // CORES
    halves = CORES
    owned = frames * local
    rows = owned * chips
    blocks = chips * halves
    same_core = [[CORES * chip + core for chip in range(chips)] for core in range(CORES)]
    partner = [(device, device ^ 1) for device in range(group)]

    def swap(value):
        return lax.all_to_all(
            value, "seq", split_axis=0, concat_axis=0, tiled=True, axis_index_groups=same_core
        )

    w_in = jnp.transpose(qkv_weight[0], (1, 0, 2))
    w_in_other = lax.ppermute(w_in, "seq", partner)
    stale = stale_kv[0].reshape(patches * frames * tokens * 2, HDIM)
    block_dims = (chips, halves, rows, HDIM)
    token_scratch = [
        pltpu.VMEM((frames, local, width), jnp.bfloat16),
        pltpu.VMEM((owned * blocks, HDIM), jnp.float32),
        pltpu.SemaphoreType.DMA((1,)),
    ]
    wide = pltpu.VMEM((chips * halves * rows, HDIM), jnp.float32)
    came = swap(call(pack_first, "pack_first", shape(*block_dims), (), (in_flight,), token_scratch, in_hbm=(0,)))
    gathered, w_out, stale = call(
        unpack_first,
        "unpack_first",
        (shape(*block_dims), shape(width, HDIM), shape(*stale.shape)),
        (),
        (came, out_weight[0], stale),
        [wide, pltpu.SemaphoreType.DMA((2,))],
        in_hbm=(1, 2),
    )
    results = []
    for tick in range(ticks):
        if tick:
            arrived = lax.ppermute(
                results[-1], "section", [(source, source + 1) for source in range(sections - 1)]
            )
            sent = call(
                functools.partial(spread, tick),
                "spread",
                shape(*block_dims),
                (),
                (entering, arrived),
                token_scratch,
                in_hbm=(0,),
            )
            gathered = call(arrange, "arrange", shape(*block_dims), (), (swap(sent),), [wide], aliases={0: 0})
        new_rows = rows if tick else first_rows(rows, stale.shape[0] // 2, width)[1]
        normed, own = call(
            functools.partial(layer_keys, tick, frames),
            "keys",
            (shape(rows, width), shape(new_rows, 2 * halves * HDIM)),
            (patch_frames,),
            (gathered, norm_gain, w_in, w_in_other) + (() if tick else (stale, w_out)),
            () if tick else [pltpu.VMEM(stale.shape, jnp.float32)],
        )
        other = lax.ppermute(own, "seq", partner)
        queries = call(layer_queries, "queries", shape(rows, halves * HDIM), (), (normed, w_in, w_in_other))
        attended, kv = call(
            functools.partial(layer_attend, tick, frames),
            "attend",
            (shape(chips, halves, rows, HDIM), shape(patches, CORES, rows, 2 * halves * HDIM)),
            (patch_frames,),
            (queries, own, other) + ((kv,) if tick else ()),
            aliases={4: 1} if tick else {},
        )
        if tick == 0:
            first_other = other
        results.append(
            call(
                functools.partial(layer_back, tick, frames, stale.shape[0] // 2),
                "back",
                shape(halves, rows, HDIM),
                (patch_frames,),
                (swap(attended), w_out, first_other, gathered),
            )
        )

    parts = ticks * halves * owned
    sent = call(
        pack_last,
        "pack_last",
        shape(chips, parts, HDIM),
        (),
        tuple(results),
        [pltpu.VMEM((ticks * halves * rows, HDIM), jnp.float32)],
    )
    outputs = call(
        unpack_last,
        "unpack_last",
        shape(patches, frames, local, width),
        (patch_frames,),
        (swap(sent),),
        [pltpu.VMEM((ticks * owned, width), jnp.float32)],
    )
    return outputs[None]


def solution(mesh):
    in_specs = (
        P("section", None, "seq", None),
        P(None, None, "seq", None),
        P(),
        P("section", None),
        P("section", None, None, "seq"),
        P("section", None, "seq"),
        P("section", None, None, None, None, "seq"),
    )
    out_specs = P("section", None, None, "seq", None)
    return jax.shard_map(
        on_device, mesh=mesh, in_specs=in_specs, out_specs=out_specs, check_vma=False
    )
```

```python
import functools
import math

import jax
import jax.numpy as jnp
from jax import lax
from jax.experimental import pallas as pl
from jax.experimental.pallas import tpu as pltpu
from jax.sharding import PartitionSpec as P

HDIM = 128
CORES = 2
WEIGHT_PARTS = 4
MOST_SECTIONS = 1024
VMEM_LIMIT = 12 * 1024 * 1024


def call(body, name, out_shape, scalars, arrays, scratch=(), in_hbm=(), aliases=()):
    arrays = [
        pltpu.with_memory_space_constraint(array, pltpu.HBM) if place in in_hbm else array
        for place, array in enumerate(arrays)
    ]
    in_vmem = pl.BlockSpec(memory_space=pltpu.VMEM)
    in_smem = pl.BlockSpec(memory_space=pltpu.SMEM)
    return pl.pallas_call(
        body,
        out_shape=out_shape,
        in_specs=[in_smem] * len(scalars)
        + [pl.BlockSpec(memory_space=pl.ANY) if place in in_hbm else in_vmem for place in range(len(arrays))],
        out_specs=jax.tree.map(lambda _: in_vmem, out_shape),
        scratch_shapes=list(scratch),
        input_output_aliases=dict(aliases),
        compiler_params=pltpu.CompilerParams(vmem_limit_bytes=VMEM_LIMIT),
        name=name,
    )(*scalars, *arrays)


def shape(*dims):
    return jax.ShapeDtypeStruct(dims, jnp.bfloat16)


def fetch_rows(tokens_any, tokens_ref, rows_ref, sem_ref):
    fetch = pltpu.make_async_copy(tokens_any, tokens_ref, sem_ref.at[0])
    fetch.start()
    fetch.wait()
    frames, local, width = tokens_ref.shape
    blocks = width // HDIM
    for frame in range(frames):
        wide = tokens_ref[frame].astype(jnp.float32)
        for block in range(blocks):
            rows_ref[pl.ds(frame * local * blocks + block, local, stride=blocks), :] = wide[
                :, block * HDIM:(block + 1) * HDIM
            ]


def send_rows(rows_ref, out_ref):
    chips, halves, tokens, _ = out_ref.shape
    for half in range(halves):
        rows = rows_ref[half * tokens:(half + 1) * tokens].astype(jnp.bfloat16)
        for chip in range(chips):
            out_ref[chip, half] = rows


def pack_first(mine_any, out_ref, mine_ref, rows_ref, sem_ref):
    fetch_rows(mine_any.at[0], mine_ref, rows_ref, sem_ref)
    send_rows(rows_ref, out_ref)


def to_blocks(came_ref, hidden_ref, wide_ref):
    chips, halves, tokens, _ = came_ref.shape
    blocks = chips * halves
    for chip in range(chips):
        for half in range(halves):
            first = (chip * halves + half) * tokens
            wide_ref[first:first + tokens] = came_ref[chip, half].astype(jnp.float32)
    for token in range(tokens // chips):
        for block in range(blocks):
            hidden_ref[block // halves, block % halves, token * chips:(token + 1) * chips] = wide_ref[
                pl.ds(token * blocks + block, chips, stride=halves * tokens), :
            ].astype(jnp.bfloat16)


def unpack_first(came_ref, weight_any, stale_any, hidden_ref, weight_ref, stale_ref, wide_ref, sem_ref):
    fetches = [
        pltpu.make_async_copy(weight_any, weight_ref, sem_ref.at[0]),
        pltpu.make_async_copy(stale_any, stale_ref, sem_ref.at[1]),
    ]
    for fetch in fetches:
        fetch.start()
    to_blocks(came_ref, hidden_ref, wide_ref)
    for fetch in fetches:
        fetch.wait()


def spread(tick, entering_any, arrived_ref, out_ref, tokens_ref, rows_ref, sem_ref):
    section = lax.axis_index("section")

    @pl.when(section == 0)
    def _():
        fetch_rows(entering_any.at[tick - 1], tokens_ref, rows_ref, sem_ref)
        send_rows(rows_ref, out_ref)

    @pl.when(section != 0)
    def _():
        for chip in range(out_ref.shape[0]):
            out_ref[chip] = arrived_ref[...]


def arrange(came_ref, hidden_ref, wide_ref):
    @pl.when(lax.axis_index("section") == 0)
    def _():
        to_blocks(came_ref, hidden_ref, wide_ref)


def slot_of(frames_ref, tick):
    slots = frames_ref.shape[0]
    return lax.rem(tick + slots * MOST_SECTIONS - lax.axis_index("section"), slots)


def own_core():
    return lax.rem(lax.axis_index("seq"), CORES)


def live_rows(frames, frames_ref, tick, rows):
    row_ids = lax.broadcasted_iota(jnp.int32, (rows, 1), 0)
    return row_ids < frames_ref[slot_of(frames_ref, tick)] * (rows // frames)


def first_rows(tokens, slot_rows, width):
    stale = tokens + slot_rows // CORES
    return stale, stale + width // WEIGHT_PARTS


def two_heads(own_ref, other_ref, kinds, span):
    return jnp.concatenate([ref[kind, span] for ref in (own_ref, other_ref) for kind in kinds], axis=1)


def layer_keys(tick, frames, frames_ref, x_ref, gain_ref, w_own_ref, w_other_ref, *refs):
    *first_refs, xn_ref, new_ref = refs if tick else refs[:-1]
    chips, halves, tokens, width = x_ref.shape
    pair = halves * width
    squares = jnp.zeros((tokens, width), jnp.float32)
    for chip in range(chips):
        for half in range(halves):
            wide = x_ref[chip, half].astype(jnp.float32)
            squares = squares + wide * wide
    mean_square = jnp.sum(squares, axis=1, keepdims=True) / (chips * pair)
    scale = jnp.where(live_rows(frames, frames_ref, tick, tokens), lax.rsqrt(mean_square + 1e-06), 0.0)
    total = jnp.zeros((tokens, 2 * pair), jnp.float32)
    for chip in range(chips):
        span = slice(chip * pair, (chip + 1) * pair)
        wide = jnp.concatenate([x_ref[chip, half] for half in range(halves)], axis=1).astype(jnp.float32)
        normed = (wide * scale * gain_ref[:, span].astype(jnp.float32)).astype(jnp.bfloat16)
        xn_ref[:, span] = normed
        total = total + jnp.dot(
            normed, two_heads(w_own_ref, w_other_ref, (1, 2), span), preferred_element_type=jnp.float32
        )
    new_ref[:tokens] = total.astype(jnp.bfloat16)
    if tick == 0:
        stale_ref, out_ref = first_refs
        wide_ref = refs[-1]
        rows = stale_ref.shape[0] // 2
        stale_end, weight_end = first_rows(tokens, rows, out_ref.shape[0])
        wide_ref[...] = stale_ref[...].astype(jnp.float32)
        each = rows // CORES
        for part in range(CORES):
            for kind in range(2):
                first = (part * 2 + kind) * width
                new_ref[tokens:stale_end, first:first + width] = wide_ref[
                    pl.ds(part * 2 * each + kind, each, stride=2), :
                ].astype(jnp.bfloat16)
        part_rows = weight_end - stale_end
        for part in range(WEIGHT_PARTS):
            new_ref[stale_end:weight_end, part * width:(part + 1) * width] = out_ref[
                part * part_rows:(part + 1) * part_rows
            ]


def layer_queries(xn_ref, w_own_ref, w_other_ref, out_ref):
    pair = out_ref.shape[1]
    total = jnp.zeros(out_ref.shape, jnp.float32)
    for first in range(0, xn_ref.shape[1], pair):
        span = slice(first, first + pair)
        total = total + jnp.dot(
            xn_ref[:, span], two_heads(w_own_ref, w_other_ref, (0,), span), preferred_element_type=jnp.float32
        )
    out_ref[...] = total.astype(jnp.bfloat16)


def layer_attend(tick, frames, frames_ref, q_ref, own_ref, other_ref, *refs):
    out_ref, kv_out = refs[-2:]
    chips, halves, tokens, width = out_ref.shape
    slots = kv_out.shape[0]
    rows = CORES * tokens
    span = tokens // frames
    both = 2 * width
    slot = slot_of(frames_ref, tick)
    core = own_core()
    if tick == 0:
        for place_of, ref in enumerate((own_ref, other_ref)):
            columns = slice(place_of * both, (place_of + 1) * both)
            for old in range(slots):
                part, place = divmod(old, slots // CORES)
                for frame in range(frames):
                    for piece in range(CORES):
                        row = tokens + place * rows + (frame * CORES + piece) * span
                        kv_out[old, piece, frame * span:(frame + 1) * span, columns] = ref[
                            row:row + span, part * both:(part + 1) * both
                        ]
    kv_out[slot, core] = own_ref[:tokens]
    kv_out[slot, 1 - core, :, :both] = other_ref[:tokens, both:]
    kv_out[slot, 1 - core, :, both:] = other_ref[:tokens, :both]
    key_ids = lax.broadcasted_iota(jnp.int32, (1, slots * rows), 1)
    limit = jnp.zeros_like(key_ids)
    for patch in range(slots):
        limit = jnp.where(key_ids // rows == patch, frames_ref[patch] * span, limit)
    key_live = key_ids % tokens < limit
    scores = []
    for head in range(halves):
        keys = kv_out[:, :, :, head * both:head * both + width].reshape(slots * rows, width)
        scores.append(
            lax.dot_general(
                q_ref[:, head * width:(head + 1) * width], keys, (((1,), (1,)), ((), ())),
                preferred_element_type=jnp.float32,
            )
        )
    scores = jnp.where(key_live, jnp.concatenate(scores, axis=0) * (1.0 / math.sqrt(HDIM)), -jnp.inf)
    exponent = jnp.exp(scores - jnp.max(scores, axis=1, keepdims=True))
    weights_low = exponent.astype(jnp.bfloat16)
    share = 1.0 / jnp.sum(exponent, axis=1, keepdims=True)
    attended = []
    for head in range(halves):
        span = slice(head * tokens, (head + 1) * tokens)
        values = kv_out[:, :, :, head * both + width:(head + 1) * both].reshape(slots * rows, width)
        weighted = jnp.dot(weights_low[span], values, preferred_element_type=jnp.float32)
        attended.append((weighted * share[span]).astype(jnp.bfloat16))
    for head, half in enumerate((core, 1 - core)):
        for chip in range(chips):
            out_ref[chip, half] = attended[head]


def layer_back(tick, frames, slot_rows, frames_ref, a_ref, w_own_ref, first_other_ref, x_ref, out_ref):
    chips, halves, tokens, width = a_ref.shape
    pair = halves * width
    chip = lax.div(lax.axis_index("seq"), CORES)
    core = own_core()
    live = live_rows(frames, frames_ref, tick, tokens)
    stale_end, weight_end = first_rows(tokens, slot_rows, w_own_ref.shape[0])
    branch = jnp.zeros((tokens, pair), jnp.float32)
    for source in range(chips):
        wide = jnp.concatenate([a_ref[source, half] for half in range(halves)], axis=1)
        part, row = divmod(source * pair, weight_end - stale_end)
        row += stale_end
        weights = jnp.concatenate(
            [
                w_own_ref[source * pair:(source + 1) * pair],
                first_other_ref[row:row + pair, part * width:(part + 1) * width],
            ],
            axis=1,
        )
        branch = branch + jnp.dot(wide, weights, preferred_element_type=jnp.float32)
    branch = branch.astype(jnp.bfloat16).astype(jnp.float32)
    for head, half in enumerate((core, 1 - core)):
        total = x_ref[chip, half].astype(jnp.float32) + branch[:, head * width:(head + 1) * width]
        out_ref[half] = jnp.where(live, total, 0.0).astype(jnp.bfloat16)


def pack_last(*refs):
    *result_refs, out_ref, wide_ref = refs
    chips, parts, _ = out_ref.shape
    ticks = len(result_refs)
    for tick, ref in enumerate(result_refs):
        halves, tokens, _ = ref.shape
        for half in range(halves):
            first = (half * ticks + tick) * tokens
            wide_ref[first:first + tokens] = ref[half].astype(jnp.float32)
    for chip in range(chips):
        out_ref[chip] = wide_ref[pl.ds(chip, parts, stride=chips), :].astype(jnp.bfloat16)


def unpack_last(frames_ref, came_ref, out_ref, turn_ref):
    chips, parts, width = came_ref.shape
    patches, frames, local, _ = out_ref.shape
    each = parts // CORES
    for chip in range(chips):
        wide = came_ref[chip].astype(jnp.float32)
        for half in range(CORES):
            first = (chip * CORES + half) * width
            turn_ref[:, first:first + width] = wide[half * each:(half + 1) * each]
    for tick in range(patches):
        slot = slot_of(frames_ref, tick)
        for frame in range(frames):
            row = (tick * frames + frame) * local
            out_ref[slot, frame] = turn_ref[row:row + local].astype(jnp.bfloat16)


def on_device(in_flight, entering, patch_frames, norm_gain, qkv_weight, out_weight, stale_kv):
    sections = lax.axis_size("section")
    group = lax.axis_size("seq")
    patches, frames, tokens = stale_kv.shape[1:4]
    local = in_flight.shape[2]
    width = in_flight.shape[3]
    ticks = patches
    chips = group // CORES
    halves = CORES
    owned = frames * local
    rows = owned * chips
    blocks = chips * halves
    same_core = [[CORES * chip + core for chip in range(chips)] for core in range(CORES)]
    partner = [(device, device ^ 1) for device in range(group)]

    def swap(value):
        return lax.all_to_all(
            value, "seq", split_axis=0, concat_axis=0, tiled=True, axis_index_groups=same_core
        )

    w_in = jnp.transpose(qkv_weight[0], (1, 0, 2))
    w_in_other = lax.ppermute(w_in, "seq", partner)
    stale = stale_kv[0].reshape(patches * frames * tokens * 2, HDIM)
    block_dims = (chips, halves, rows, HDIM)
    token_scratch = [
        pltpu.VMEM((frames, local, width), jnp.bfloat16),
        pltpu.VMEM((owned * blocks, HDIM), jnp.float32),
        pltpu.SemaphoreType.DMA((1,)),
    ]
    wide = pltpu.VMEM((chips * halves * rows, HDIM), jnp.float32)
    came = swap(call(pack_first, "pack_first", shape(*block_dims), (), (in_flight,), token_scratch, in_hbm=(0,)))
    gathered, w_out, stale = call(
        unpack_first,
        "unpack_first",
        (shape(*block_dims), shape(width, HDIM), shape(*stale.shape)),
        (),
        (came, out_weight[0], stale),
        [wide, pltpu.SemaphoreType.DMA((2,))],
        in_hbm=(1, 2),
    )
    results = []
    for tick in range(ticks):
        if tick:
            arrived = lax.ppermute(
                results[-1], "section", [(source, source + 1) for source in range(sections - 1)]
            )
            sent = call(
                functools.partial(spread, tick),
                "spread",
                shape(*block_dims),
                (),
                (entering, arrived),
                token_scratch,
                in_hbm=(0,),
            )
            gathered = call(arrange, "arrange", shape(*block_dims), (), (swap(sent),), [wide], aliases={0: 0})
        new_rows = rows if tick else first_rows(rows, stale.shape[0] // 2, width)[1]
        normed, own = call(
            functools.partial(layer_keys, tick, frames),
            "keys",
            (shape(rows, width), shape(new_rows, 2 * halves * HDIM)),
            (patch_frames,),
            (gathered, norm_gain, w_in, w_in_other) + (() if tick else (stale, w_out)),
            () if tick else [pltpu.VMEM(stale.shape, jnp.float32)],
        )
        other = lax.ppermute(own, "seq", partner)
        queries = call(layer_queries, "queries", shape(rows, halves * HDIM), (), (normed, w_in, w_in_other))
        attended, kv = call(
            functools.partial(layer_attend, tick, frames),
            "attend",
            (shape(chips, halves, rows, HDIM), shape(patches, CORES, rows, 2 * halves * HDIM)),
            (patch_frames,),
            (queries, own, other) + ((kv,) if tick else ()),
            aliases={4: 1} if tick else {},
        )
        if tick == 0:
            first_other = other
        results.append(
            call(
                functools.partial(layer_back, tick, frames, stale.shape[0] // 2),
                "back",
                shape(halves, rows, HDIM),
                (patch_frames,),
                (swap(attended), w_out, first_other, gathered),
            )
        )

    parts = ticks * halves * owned
    sent = call(
        pack_last,
        "pack_last",
        shape(chips, parts, HDIM),
        (),
        tuple(results),
        [pltpu.VMEM((ticks * halves * rows, HDIM), jnp.float32)],
    )
    outputs = call(
        unpack_last,
        "unpack_last",
        shape(patches, frames, local, width),
        (patch_frames,),
        (swap(sent),),
        [pltpu.VMEM((ticks * owned, width), jnp.float32)],
    )
    return outputs[None]


def solution(mesh):
    in_specs = (
        P("section", None, "seq", None),
        P(None, None, "seq", None),
        P(),
        P("section", None),
        P("section", None, None, "seq"),
        P("section", None, "seq"),
        P("section", None, None, None, None, "seq"),
    )
    out_specs = P("section", None, None, "seq", None)
    return jax.shard_map(
        on_device, mesh=mesh, in_specs=in_specs, out_specs=out_specs, check_vma=False
    )
```

```python
import functools
import math

import jax
import jax.numpy as jnp
from jax import lax
from jax.experimental import pallas as pl
from jax.experimental.pallas import tpu as pltpu
from jax.sharding import PartitionSpec as P

HDIM = 128
CORES = 2
WEIGHT_PARTS = 4
SUBLANES = 8
MOST_SECTIONS = 1024
VMEM_LIMIT = 12 * 1024 * 1024


def call(body, name, out_shape, scalars, arrays, scratch=(), in_hbm=(), aliases=()):
    arrays = [
        pltpu.with_memory_space_constraint(array, pltpu.HBM) if place in in_hbm else array
        for place, array in enumerate(arrays)
    ]
    in_vmem = pl.BlockSpec(memory_space=pltpu.VMEM)
    in_smem = pl.BlockSpec(memory_space=pltpu.SMEM)
    return pl.pallas_call(
        body,
        out_shape=out_shape,
        in_specs=[in_smem] * len(scalars)
        + [pl.BlockSpec(memory_space=pl.ANY) if place in in_hbm else in_vmem for place in range(len(arrays))],
        out_specs=jax.tree.map(lambda _: in_vmem, out_shape),
        scratch_shapes=list(scratch),
        input_output_aliases=dict(aliases),
        compiler_params=pltpu.CompilerParams(vmem_limit_bytes=VMEM_LIMIT),
        name=name,
    )(*scalars, *arrays)


def shape(*dims):
    return jax.ShapeDtypeStruct(dims, jnp.bfloat16)


def fetch_rows(tokens_any, tokens_ref, rows_ref, sem_ref):
    fetch = pltpu.make_async_copy(tokens_any, tokens_ref, sem_ref.at[0])
    fetch.start()
    fetch.wait()
    frames, local, width = tokens_ref.shape
    blocks = width // HDIM
    for frame in range(frames):
        wide = tokens_ref[frame].astype(jnp.float32)
        for block in range(blocks):
            rows_ref[pl.ds(frame * local * blocks + block, local, stride=blocks), :] = wide[
                :, block * HDIM:(block + 1) * HDIM
            ]


def send_rows(rows_ref, out_ref):
    chips, halves, tokens, _ = out_ref.shape
    for half in range(halves):
        rows = rows_ref[half * tokens:(half + 1) * tokens].astype(jnp.bfloat16)
        for chip in range(chips):
            out_ref[chip, half] = rows


def pack_first(mine_any, out_ref, mine_ref, rows_ref, sem_ref):
    fetch_rows(mine_any.at[0], mine_ref, rows_ref, sem_ref)
    send_rows(rows_ref, out_ref)


def to_blocks(came_ref, hidden_ref, wide_ref):
    chips, halves, tokens, _ = came_ref.shape
    blocks = chips * halves
    for chip in range(chips):
        for half in range(halves):
            first = (chip * halves + half) * tokens
            wide_ref[first:first + tokens] = came_ref[chip, half].astype(jnp.float32)
    for token in range(tokens // chips):
        for block in range(blocks):
            hidden_ref[block // halves, block % halves, token * chips:(token + 1) * chips] = wide_ref[
                pl.ds(token * blocks + block, chips, stride=halves * tokens), :
            ].astype(jnp.bfloat16)


def unpack_first(came_ref, weight_any, stale_any, hidden_ref, weight_ref, stale_ref, wide_ref, sem_ref):
    fetches = [
        pltpu.make_async_copy(weight_any, weight_ref, sem_ref.at[0]),
        pltpu.make_async_copy(stale_any, stale_ref, sem_ref.at[1]),
    ]
    for fetch in fetches:
        fetch.start()
    to_blocks(came_ref, hidden_ref, wide_ref)
    for fetch in fetches:
        fetch.wait()


def spread(tick, entering_any, arrived_ref, out_ref, tokens_ref, rows_ref, sem_ref):
    section = lax.axis_index("section")

    @pl.when(section == 0)
    def _():
        fetch_rows(entering_any.at[tick - 1], tokens_ref, rows_ref, sem_ref)
        send_rows(rows_ref, out_ref)

    @pl.when(section != 0)
    def _():
        for chip in range(out_ref.shape[0]):
            out_ref[chip] = arrived_ref[...]


def arrange(came_ref, hidden_ref, wide_ref):
    @pl.when(lax.axis_index("section") == 0)
    def _():
        to_blocks(came_ref, hidden_ref, wide_ref)


def slot_of(frames_ref, tick):
    slots = frames_ref.shape[0]
    return lax.rem(tick + slots * MOST_SECTIONS - lax.axis_index("section"), slots)


def own_core():
    return lax.rem(lax.axis_index("seq"), CORES)


def live_rows(frames, frames_ref, tick, rows):
    row_ids = lax.broadcasted_iota(jnp.int32, (rows, 1), 0)
    return row_ids < frames_ref[slot_of(frames_ref, tick)] * (rows // frames)


def first_rows(tokens, slot_rows, width):
    stale = tokens + slot_rows // CORES
    return stale, stale + width // WEIGHT_PARTS


def two_heads(own_ref, other_ref, kinds, span):
    return jnp.concatenate([ref[kind, span] for ref in (own_ref, other_ref) for kind in kinds], axis=1)


def layer_keys(tick, frames, frames_ref, x_ref, gain_ref, w_own_ref, w_other_ref, *refs):
    *first_refs, xn_ref, new_ref = refs if tick else refs[:-1]
    chips, halves, tokens, width = x_ref.shape
    pair = halves * width
    squares = jnp.zeros((tokens, width), jnp.float32)
    for chip in range(chips):
        for half in range(halves):
            wide = x_ref[chip, half].astype(jnp.float32)
            squares = squares + wide * wide
    mean_square = jnp.sum(squares, axis=1, keepdims=True) / (chips * pair)
    scale = jnp.where(live_rows(frames, frames_ref, tick, tokens), lax.rsqrt(mean_square + 1e-06), 0.0)
    total = jnp.zeros((tokens, 2 * pair), jnp.float32)
    for chip in range(chips):
        span = slice(chip * pair, (chip + 1) * pair)
        wide = jnp.concatenate([x_ref[chip, half] for half in range(halves)], axis=1).astype(jnp.float32)
        normed = (wide * scale * gain_ref[:, span].astype(jnp.float32)).astype(jnp.bfloat16)
        xn_ref[:, span] = normed
        total = total + jnp.dot(
            normed, two_heads(w_own_ref, w_other_ref, (1, 2), span), preferred_element_type=jnp.float32
        )
    new_ref[:tokens] = total.astype(jnp.bfloat16)
    if tick == 0:
        stale_ref, out_ref = first_refs
        wide_ref = refs[-1]
        rows = stale_ref.shape[0] // 2
        stale_end, weight_end = first_rows(tokens, rows, out_ref.shape[0])
        wide_ref[...] = stale_ref[...].astype(jnp.float32)
        each = rows // CORES
        for part in range(CORES):
            for kind in range(2):
                first = (part * 2 + kind) * width
                new_ref[tokens:stale_end, first:first + width] = wide_ref[
                    pl.ds(part * 2 * each + kind, each, stride=2), :
                ].astype(jnp.bfloat16)
        part_rows = weight_end - stale_end
        for part in range(WEIGHT_PARTS):
            new_ref[stale_end:weight_end, part * width:(part + 1) * width] = out_ref[
                part * part_rows:(part + 1) * part_rows
            ]


def layer_queries(xn_ref, w_own_ref, w_other_ref, out_ref):
    pair = out_ref.shape[1]
    total = jnp.zeros(out_ref.shape, jnp.float32)
    for first in range(0, xn_ref.shape[1], pair):
        span = slice(first, first + pair)
        total = total + jnp.dot(
            xn_ref[:, span], two_heads(w_own_ref, w_other_ref, (0,), span), preferred_element_type=jnp.float32
        )
    out_ref[...] = total.astype(jnp.bfloat16)


def layer_attend(tick, frames, frames_ref, q_ref, own_ref, other_ref, *refs):
    out_ref, kv_out = refs[-2:]
    chips, halves, tokens, width = out_ref.shape
    slots = kv_out.shape[0]
    rows = CORES * tokens
    span = tokens // frames
    both = 2 * width
    slot = slot_of(frames_ref, tick)
    core = own_core()
    if tick == 0:
        for place_of, ref in enumerate((own_ref, other_ref)):
            columns = slice(place_of * both, (place_of + 1) * both)
            for old in range(slots):
                part, place = divmod(old, slots // CORES)
                for frame in range(frames):
                    for piece in range(CORES):
                        row = tokens + place * rows + (frame * CORES + piece) * span
                        kv_out[old, piece, frame * span:(frame + 1) * span, columns] = ref[
                            row:row + span, part * both:(part + 1) * both
                        ]
    kv_out[slot, core] = own_ref[:tokens]
    kv_out[slot, 1 - core, :, :both] = other_ref[:tokens, both:]
    kv_out[slot, 1 - core, :, both:] = other_ref[:tokens, :both]
    key_ids = lax.broadcasted_iota(jnp.int32, (1, slots * rows), 1)
    limit = jnp.zeros_like(key_ids)
    for patch in range(slots):
        limit = jnp.where(key_ids // rows == patch, frames_ref[patch] * span, limit)
    key_live = key_ids % tokens < limit
    scores = []
    for head in range(halves):
        keys = kv_out[:, :, :, head * both:head * both + width].reshape(slots * rows, width)
        scores.append(
            lax.dot_general(
                q_ref[:, head * width:(head + 1) * width], keys, (((1,), (1,)), ((), ())),
                preferred_element_type=jnp.float32,
            )
        )
    scores = jnp.where(key_live, jnp.concatenate(scores, axis=0) * (1.0 / math.sqrt(HDIM)), -jnp.inf)
    exponent = jnp.exp(scores - jnp.max(scores, axis=1, keepdims=True))
    weights_low = exponent.astype(jnp.bfloat16)
    share = 1.0 / jnp.sum(exponent, axis=1, keepdims=True)
    attended = []
    for head in range(halves):
        span = slice(head * tokens, (head + 1) * tokens)
        values = kv_out[:, :, :, head * both + width:(head + 1) * both].reshape(slots * rows, width)
        weighted = jnp.dot(weights_low[span], values, preferred_element_type=jnp.float32)
        attended.append((weighted * share[span]).astype(jnp.bfloat16))
    for head, half in enumerate((core, 1 - core)):
        for chip in range(chips):
            out_ref[chip, half] = attended[head]


def layer_back(tick, frames, slot_rows, frames_ref, a_ref, w_own_ref, first_other_ref, x_ref, out_ref):
    chips, halves, tokens, width = a_ref.shape
    pair = halves * width
    chip = lax.div(lax.axis_index("seq"), CORES)
    core = own_core()
    live = live_rows(frames, frames_ref, tick, tokens)
    stale_end, weight_end = first_rows(tokens, slot_rows, w_own_ref.shape[0])
    branch = jnp.zeros((tokens, pair), jnp.float32)
    for source in range(chips):
        wide = jnp.concatenate([a_ref[source, half] for half in range(halves)], axis=1)
        part, row = divmod(source * pair, weight_end - stale_end)
        row += stale_end
        weights = jnp.concatenate(
            [
                w_own_ref[source * pair:(source + 1) * pair],
                first_other_ref[row:row + pair, part * width:(part + 1) * width],
            ],
            axis=1,
        )
        branch = branch + jnp.dot(wide, weights, preferred_element_type=jnp.float32)
    branch = branch.astype(jnp.bfloat16).astype(jnp.float32)
    for head, half in enumerate((core, 1 - core)):
        total = x_ref[chip, half].astype(jnp.float32) + branch[:, head * width:(head + 1) * width]
        out_ref[half] = jnp.where(live, total, 0.0).astype(jnp.bfloat16)


def pack_last(*refs):
    *result_refs, out_ref, wide_ref = refs
    chips, parts, _ = out_ref.shape
    ticks = len(result_refs)
    for tick, ref in enumerate(result_refs):
        halves, tokens, _ = ref.shape
        for half in range(halves):
            first = (half * ticks + tick) * tokens
            wide_ref[first:first + tokens] = ref[half].astype(jnp.float32)
    for chip in range(chips):
        out_ref[chip] = wide_ref[pl.ds(chip, parts, stride=chips), :].astype(jnp.bfloat16)


def unpack_last(frames_ref, came_ref, out_ref, turn_ref):
    chips, parts, width = came_ref.shape
    patches, frames, local, _ = out_ref.shape
    each = parts // CORES
    for chip in range(chips):
        wide = came_ref[chip].astype(jnp.float32)
        for half in range(CORES):
            first = (chip * CORES + half) * width
            turn_ref[:each, first:first + width] = wide[half * each:(half + 1) * each]
    for tick in range(patches):
        slot = slot_of(frames_ref, tick)
        for frame in range(frames):
            row = (tick * frames + frame) * local
            out_ref[slot, frame] = turn_ref[row:row + local].astype(jnp.bfloat16)


def on_device(in_flight, entering, patch_frames, norm_gain, qkv_weight, out_weight, stale_kv):
    sections = lax.axis_size("section")
    group = lax.axis_size("seq")
    patches, frames, tokens = stale_kv.shape[1:4]
    local = in_flight.shape[2]
    width = in_flight.shape[3]
    ticks = patches
    chips = group // CORES
    halves = CORES
    owned = frames * local
    rows = owned * chips
    blocks = chips * halves
    same_core = [[CORES * chip + core for chip in range(chips)] for core in range(CORES)]
    partner = [(device, device ^ 1) for device in range(group)]

    def swap(value):
        return lax.all_to_all(
            value, "seq", split_axis=0, concat_axis=0, tiled=True, axis_index_groups=same_core
        )

    w_in = jnp.transpose(qkv_weight[0], (1, 0, 2))
    w_in_other = lax.ppermute(w_in, "seq", partner)
    stale = stale_kv[0].reshape(patches * frames * tokens * 2, HDIM)
    block_dims = (chips, halves, rows, HDIM)
    token_scratch = [
        pltpu.VMEM((frames, local, width), jnp.bfloat16),
        pltpu.VMEM(((owned + SUBLANES) * blocks, HDIM), jnp.float32),
        pltpu.SemaphoreType.DMA((1,)),
    ]
    wide = pltpu.VMEM((chips * halves * rows, HDIM), jnp.float32)
    came = swap(call(pack_first, "pack_first", shape(*block_dims), (), (in_flight,), token_scratch, in_hbm=(0,)))
    gathered, w_out, stale = call(
        unpack_first,
        "unpack_first",
        (shape(*block_dims), shape(width, HDIM), shape(*stale.shape)),
        (),
        (came, out_weight[0], stale),
        [wide, pltpu.SemaphoreType.DMA((2,))],
        in_hbm=(1, 2),
    )
    results = []
    for tick in range(ticks):
        if tick:
            arrived = lax.ppermute(
                results[-1], "section", [(source, source + 1) for source in range(sections - 1)]
            )
            sent = call(
                functools.partial(spread, tick),
                "spread",
                shape(*block_dims),
                (),
                (entering, arrived),
                token_scratch,
                in_hbm=(0,),
            )
            gathered = call(arrange, "arrange", shape(*block_dims), (), (swap(sent),), [wide], aliases={0: 0})
        new_rows = rows if tick else first_rows(rows, stale.shape[0] // 2, width)[1]
        normed, own = call(
            functools.partial(layer_keys, tick, frames),
            "keys",
            (shape(rows, width), shape(new_rows, 2 * halves * HDIM)),
            (patch_frames,),
            (gathered, norm_gain, w_in, w_in_other) + (() if tick else (stale, w_out)),
            () if tick else [pltpu.VMEM(stale.shape, jnp.float32)],
        )
        other = lax.ppermute(own, "seq", partner)
        queries = call(layer_queries, "queries", shape(rows, halves * HDIM), (), (normed, w_in, w_in_other))
        attended, kv = call(
            functools.partial(layer_attend, tick, frames),
            "attend",
            (shape(chips, halves, rows, HDIM), shape(patches, CORES, rows, 2 * halves * HDIM)),
            (patch_frames,),
            (queries, own, other) + ((kv,) if tick else ()),
            aliases={4: 1} if tick else {},
        )
        if tick == 0:
            first_other = other
        results.append(
            call(
                functools.partial(layer_back, tick, frames, stale.shape[0] // 2),
                "back",
                shape(halves, rows, HDIM),
                (patch_frames,),
                (swap(attended), w_out, first_other, gathered),
            )
        )

    parts = ticks * halves * owned
    sent = call(
        pack_last,
        "pack_last",
        shape(chips, parts, HDIM),
        (),
        tuple(results),
        [pltpu.VMEM((ticks * halves * rows, HDIM), jnp.float32)],
    )
    outputs = call(
        unpack_last,
        "unpack_last",
        shape(patches, frames, local, width),
        (patch_frames,),
        (swap(sent),),
        [pltpu.VMEM((ticks * owned + SUBLANES, width), jnp.float32)],
    )
    return outputs[None]


def solution(mesh):
    in_specs = (
        P("section", None, "seq", None),
        P(None, None, "seq", None),
        P(),
        P("section", None),
        P("section", None, None, "seq"),
        P("section", None, "seq"),
        P("section", None, None, None, None, "seq"),
    )
    out_specs = P("section", None, None, "seq", None)
    return jax.shard_map(
        on_device, mesh=mesh, in_specs=in_specs, out_specs=out_specs, check_vma=False
    )
```

```python
import functools
import math

import jax
import jax.numpy as jnp
from jax import lax
from jax.experimental import pallas as pl
from jax.experimental.pallas import tpu as pltpu
from jax.sharding import PartitionSpec as P

HDIM = 128
CORES = 2
WEIGHT_PARTS = 4
SUBLANES = 8
MOST_SECTIONS = 1024
VMEM_LIMIT = 12 * 1024 * 1024


def call(body, name, out_shape, scalars, arrays, scratch=(), in_hbm=(), aliases=()):
    arrays = [
        pltpu.with_memory_space_constraint(array, pltpu.HBM) if place in in_hbm else array
        for place, array in enumerate(arrays)
    ]
    in_vmem = pl.BlockSpec(memory_space=pltpu.VMEM)
    in_smem = pl.BlockSpec(memory_space=pltpu.SMEM)
    return pl.pallas_call(
        body,
        out_shape=out_shape,
        in_specs=[in_smem] * len(scalars)
        + [pl.BlockSpec(memory_space=pl.ANY) if place in in_hbm else in_vmem for place in range(len(arrays))],
        out_specs=jax.tree.map(lambda _: in_vmem, out_shape),
        scratch_shapes=list(scratch),
        input_output_aliases=dict(aliases),
        compiler_params=pltpu.CompilerParams(vmem_limit_bytes=VMEM_LIMIT),
        name=name,
    )(*scalars, *arrays)


def shape(*dims):
    return jax.ShapeDtypeStruct(dims, jnp.bfloat16)


def fetch_rows(tokens_any, tokens_ref, rows_ref, sem_ref):
    fetch = pltpu.make_async_copy(tokens_any, tokens_ref, sem_ref.at[0])
    fetch.start()
    fetch.wait()
    frames, local, width = tokens_ref.shape
    blocks = width // HDIM
    for frame in range(frames):
        wide = tokens_ref[frame].astype(jnp.float32)
        for block in range(blocks):
            rows_ref[pl.ds(frame * local * blocks + block, local, stride=blocks), :] = wide[
                :, block * HDIM:(block + 1) * HDIM
            ]


def send_rows(rows_ref, out_ref):
    chips, halves, tokens, _ = out_ref.shape
    for half in range(halves):
        rows = rows_ref[half * tokens:(half + 1) * tokens].astype(jnp.bfloat16)
        for chip in range(chips):
            out_ref[chip, half] = rows


def pack_first(mine_any, out_ref, mine_ref, rows_ref, sem_ref):
    fetch_rows(mine_any.at[0], mine_ref, rows_ref, sem_ref)
    send_rows(rows_ref, out_ref)


def to_blocks(came_ref, hidden_ref, wide_ref):
    chips, halves, tokens, _ = came_ref.shape
    blocks = chips * halves
    for chip in range(chips):
        for half in range(halves):
            first = (chip * halves + half) * tokens
            wide_ref[first:first + tokens] = came_ref[chip, half].astype(jnp.float32)
    for token in range(tokens // chips):
        for block in range(blocks):
            hidden_ref[block // halves, block % halves, token * chips:(token + 1) * chips] = wide_ref[
                pl.ds(token * blocks + block, chips, stride=halves * tokens), :
            ].astype(jnp.bfloat16)


def unpack_first(came_ref, weight_any, stale_any, hidden_ref, weight_ref, stale_ref, wide_ref, sem_ref):
    fetches = [
        pltpu.make_async_copy(weight_any, weight_ref, sem_ref.at[0]),
        pltpu.make_async_copy(stale_any, stale_ref, sem_ref.at[1]),
    ]
    for fetch in fetches:
        fetch.start()
    to_blocks(came_ref, hidden_ref, wide_ref)
    for fetch in fetches:
        fetch.wait()


def spread(tick, entering_any, arrived_ref, out_ref, tokens_ref, rows_ref, sem_ref):
    section = lax.axis_index("section")

    @pl.when(section == 0)
    def _():
        fetch_rows(entering_any.at[tick - 1], tokens_ref, rows_ref, sem_ref)
        send_rows(rows_ref, out_ref)

    @pl.when(section != 0)
    def _():
        for chip in range(out_ref.shape[0]):
            out_ref[chip] = arrived_ref[...]


def arrange(came_ref, hidden_ref, wide_ref):
    @pl.when(lax.axis_index("section") == 0)
    def _():
        to_blocks(came_ref, hidden_ref, wide_ref)


def slot_of(frames_ref, tick):
    slots = frames_ref.shape[0]
    return lax.rem(tick + slots * MOST_SECTIONS - lax.axis_index("section"), slots)


def own_core():
    return lax.rem(lax.axis_index("seq"), CORES)


def live_rows(frames, frames_ref, tick, rows):
    row_ids = lax.broadcasted_iota(jnp.int32, (rows, 1), 0)
    return row_ids < frames_ref[slot_of(frames_ref, tick)] * (rows // frames)


def first_rows(tokens, slot_rows, width):
    stale = tokens + slot_rows // CORES
    return stale, stale + width // WEIGHT_PARTS


def two_heads(own_ref, other_ref, kinds, span):
    return jnp.concatenate([ref[kind, span] for ref in (own_ref, other_ref) for kind in kinds], axis=1)


def layer_keys(tick, frames, frames_ref, x_ref, gain_ref, w_own_ref, w_other_ref, *refs):
    *first_refs, q_ref, both_ref, xn_ref = refs if tick else refs[:-1]
    new_ref = both_ref.at[0]
    chips, halves, tokens, width = x_ref.shape
    pair = halves * width
    squares = jnp.zeros((tokens, width), jnp.float32)
    for chip in range(chips):
        for half in range(halves):
            wide = x_ref[chip, half].astype(jnp.float32)
            squares = squares + wide * wide
    mean_square = jnp.sum(squares, axis=1, keepdims=True) / (chips * pair)
    scale = jnp.where(live_rows(frames, frames_ref, tick, tokens), lax.rsqrt(mean_square + 1e-06), 0.0)
    total = jnp.zeros((tokens, 2 * pair), jnp.float32)
    for chip in range(chips):
        span = slice(chip * pair, (chip + 1) * pair)
        wide = jnp.concatenate([x_ref[chip, half] for half in range(halves)], axis=1).astype(jnp.float32)
        normed = (wide * scale * gain_ref[:, span].astype(jnp.float32)).astype(jnp.bfloat16)
        xn_ref[:, span] = normed
        total = total + jnp.dot(
            normed, two_heads(w_own_ref, w_other_ref, (1, 2), span), preferred_element_type=jnp.float32
        )
    new_ref[:tokens] = total.astype(jnp.bfloat16)
    if tick == 0:
        stale_ref, out_ref = first_refs
        wide_ref = refs[-1]
        rows = stale_ref.shape[0] // 2
        stale_end, weight_end = first_rows(tokens, rows, out_ref.shape[0])
        wide_ref[...] = stale_ref[...].astype(jnp.float32)
        each = rows // CORES
        for part in range(CORES):
            for kind in range(2):
                first = (part * 2 + kind) * width
                new_ref[tokens:stale_end, first:first + width] = wide_ref[
                    pl.ds(part * 2 * each + kind, each, stride=2), :
                ].astype(jnp.bfloat16)
        part_rows = weight_end - stale_end
        for part in range(WEIGHT_PARTS):
            new_ref[stale_end:weight_end, part * width:(part + 1) * width] = out_ref[
                part * part_rows:(part + 1) * part_rows
            ]
    both_ref[1] = both_ref[0]
    total = jnp.zeros(q_ref.shape, jnp.float32)
    for chip in range(chips):
        span = slice(chip * pair, (chip + 1) * pair)
        total = total + jnp.dot(
            xn_ref[:, span], two_heads(w_own_ref, w_other_ref, (0,), span), preferred_element_type=jnp.float32
        )
    q_ref[...] = total.astype(jnp.bfloat16)


def layer_attend(tick, frames, frames_ref, q_ref, both_ref, came_ref, *refs):
    out_ref, kv_out = refs[-2:]
    chips, halves, tokens, width = out_ref.shape
    slots = kv_out.shape[0]
    rows = CORES * tokens
    span = tokens // frames
    both = 2 * width
    slot = slot_of(frames_ref, tick)
    core = own_core()
    own_ref, other_ref = both_ref.at[0], came_ref.at[1 - core]
    if tick == 0:
        for place_of, ref in enumerate((own_ref, other_ref)):
            columns = slice(place_of * both, (place_of + 1) * both)
            for old in range(slots):
                part, place = divmod(old, slots // CORES)
                for frame in range(frames):
                    for piece in range(CORES):
                        row = tokens + place * rows + (frame * CORES + piece) * span
                        kv_out[old, piece, frame * span:(frame + 1) * span, columns] = ref[
                            row:row + span, part * both:(part + 1) * both
                        ]
    kv_out[slot, core] = own_ref[:tokens]
    kv_out[slot, 1 - core, :, :both] = other_ref[:tokens, both:]
    kv_out[slot, 1 - core, :, both:] = other_ref[:tokens, :both]
    key_ids = lax.broadcasted_iota(jnp.int32, (1, slots * rows), 1)
    limit = jnp.zeros_like(key_ids)
    for patch in range(slots):
        limit = jnp.where(key_ids // rows == patch, frames_ref[patch] * span, limit)
    key_live = key_ids % tokens < limit
    scores = []
    for head in range(halves):
        keys = kv_out[:, :, :, head * both:head * both + width].reshape(slots * rows, width)
        scores.append(
            lax.dot_general(
                q_ref[:, head * width:(head + 1) * width], keys, (((1,), (1,)), ((), ())),
                preferred_element_type=jnp.float32,
            )
        )
    scores = jnp.where(key_live, jnp.concatenate(scores, axis=0) * (1.0 / math.sqrt(HDIM)), -jnp.inf)
    exponent = jnp.exp(scores - jnp.max(scores, axis=1, keepdims=True))
    weights_low = exponent.astype(jnp.bfloat16)
    share = 1.0 / jnp.sum(exponent, axis=1, keepdims=True)
    attended = []
    for head in range(halves):
        span = slice(head * tokens, (head + 1) * tokens)
        values = kv_out[:, :, :, head * both + width:(head + 1) * both].reshape(slots * rows, width)
        weighted = jnp.dot(weights_low[span], values, preferred_element_type=jnp.float32)
        attended.append((weighted * share[span]).astype(jnp.bfloat16))
    for head, half in enumerate((core, 1 - core)):
        for chip in range(chips):
            out_ref[chip, half] = attended[head]


def layer_back(tick, frames, slot_rows, frames_ref, a_ref, w_own_ref, first_came_ref, x_ref, out_ref):
    chips, halves, tokens, width = a_ref.shape
    pair = halves * width
    chip = lax.div(lax.axis_index("seq"), CORES)
    core = own_core()
    first_other_ref = first_came_ref.at[1 - core]
    live = live_rows(frames, frames_ref, tick, tokens)
    stale_end, weight_end = first_rows(tokens, slot_rows, w_own_ref.shape[0])
    branch = jnp.zeros((tokens, pair), jnp.float32)
    for source in range(chips):
        wide = jnp.concatenate([a_ref[source, half] for half in range(halves)], axis=1)
        part, row = divmod(source * pair, weight_end - stale_end)
        row += stale_end
        weights = jnp.concatenate(
            [
                w_own_ref[source * pair:(source + 1) * pair],
                first_other_ref[row:row + pair, part * width:(part + 1) * width],
            ],
            axis=1,
        )
        branch = branch + jnp.dot(wide, weights, preferred_element_type=jnp.float32)
    branch = branch.astype(jnp.bfloat16).astype(jnp.float32)
    for head, half in enumerate((core, 1 - core)):
        total = x_ref[chip, half].astype(jnp.float32) + branch[:, head * width:(head + 1) * width]
        out_ref[half] = jnp.where(live, total, 0.0).astype(jnp.bfloat16)


def pack_last(*refs):
    *result_refs, out_ref, wide_ref = refs
    chips, parts, _ = out_ref.shape
    ticks = len(result_refs)
    for tick, ref in enumerate(result_refs):
        halves, tokens, _ = ref.shape
        for half in range(halves):
            first = (half * ticks + tick) * tokens
            wide_ref[first:first + tokens] = ref[half].astype(jnp.float32)
    for chip in range(chips):
        out_ref[chip] = wide_ref[pl.ds(chip, parts, stride=chips), :].astype(jnp.bfloat16)


def unpack_last(frames_ref, came_ref, out_ref, turn_ref):
    chips, parts, width = came_ref.shape
    patches, frames, local, _ = out_ref.shape
    each = parts // CORES
    for chip in range(chips):
        wide = came_ref[chip].astype(jnp.float32)
        for half in range(CORES):
            first = (chip * CORES + half) * width
            turn_ref[:each, first:first + width] = wide[half * each:(half + 1) * each]
    for tick in range(patches):
        slot = slot_of(frames_ref, tick)
        for frame in range(frames):
            row = (tick * frames + frame) * local
            out_ref[slot, frame] = turn_ref[row:row + local].astype(jnp.bfloat16)


def on_device(in_flight, entering, patch_frames, norm_gain, qkv_weight, out_weight, stale_kv):
    sections = lax.axis_size("section")
    group = lax.axis_size("seq")
    patches, frames, tokens = stale_kv.shape[1:4]
    local = in_flight.shape[2]
    width = in_flight.shape[3]
    ticks = patches
    chips = group // CORES
    halves = CORES
    owned = frames * local
    rows = owned * chips
    blocks = chips * halves
    same_core = [[CORES * chip + core for chip in range(chips)] for core in range(CORES)]
    same_chip = [[CORES * chip + core for core in range(CORES)] for chip in range(chips)]
    partner = [(device, device ^ 1) for device in range(group)]

    def swap(value):
        return lax.all_to_all(
            value, "seq", split_axis=0, concat_axis=0, tiled=True, axis_index_groups=same_core
        )

    w_in = jnp.transpose(qkv_weight[0], (1, 0, 2))
    w_in_other = lax.ppermute(w_in, "seq", partner)
    stale = stale_kv[0].reshape(patches * frames * tokens * 2, HDIM)
    block_dims = (chips, halves, rows, HDIM)
    token_scratch = [
        pltpu.VMEM((frames, local, width), jnp.bfloat16),
        pltpu.VMEM(((owned + SUBLANES) * blocks, HDIM), jnp.float32),
        pltpu.SemaphoreType.DMA((1,)),
    ]
    wide = pltpu.VMEM((chips * halves * rows, HDIM), jnp.float32)
    came = swap(call(pack_first, "pack_first", shape(*block_dims), (), (in_flight,), token_scratch, in_hbm=(0,)))
    gathered, w_out, stale = call(
        unpack_first,
        "unpack_first",
        (shape(*block_dims), shape(width, HDIM), shape(*stale.shape)),
        (),
        (came, out_weight[0], stale),
        [wide, pltpu.SemaphoreType.DMA((2,))],
        in_hbm=(1, 2),
    )
    results = []
    for tick in range(ticks):
        if tick:
            arrived = lax.ppermute(
                results[-1], "section", [(source, source + 1) for source in range(sections - 1)]
            )
            sent = call(
                functools.partial(spread, tick),
                "spread",
                shape(*block_dims),
                (),
                (entering, arrived),
                token_scratch,
                in_hbm=(0,),
            )
            gathered = call(arrange, "arrange", shape(*block_dims), (), (swap(sent),), [wide], aliases={0: 0})
        new_rows = rows if tick else first_rows(rows, stale.shape[0] // 2, width)[1]
        queries, own = call(
            functools.partial(layer_keys, tick, frames),
            "keys",
            (shape(rows, halves * HDIM), shape(CORES, new_rows, 2 * halves * HDIM)),
            (patch_frames,),
            (gathered, norm_gain, w_in, w_in_other) + (() if tick else (stale, w_out)),
            [pltpu.VMEM((rows, width), jnp.bfloat16)] + ([] if tick else [pltpu.VMEM(stale.shape, jnp.float32)]),
        )
        other = lax.all_to_all(own, "seq", split_axis=0, concat_axis=0, tiled=True, axis_index_groups=same_chip)
        attended, kv = call(
            functools.partial(layer_attend, tick, frames),
            "attend",
            (shape(chips, halves, rows, HDIM), shape(patches, CORES, rows, 2 * halves * HDIM)),
            (patch_frames,),
            (queries, own, other) + ((kv,) if tick else ()),
            aliases={4: 1} if tick else {},
        )
        if tick == 0:
            first_other = other
        results.append(
            call(
                functools.partial(layer_back, tick, frames, stale.shape[0] // 2),
                "back",
                shape(halves, rows, HDIM),
                (patch_frames,),
                (swap(attended), w_out, first_other, gathered),
            )
        )

    parts = ticks * halves * owned
    sent = call(
        pack_last,
        "pack_last",
        shape(chips, parts, HDIM),
        (),
        tuple(results),
        [pltpu.VMEM((ticks * halves * rows, HDIM), jnp.float32)],
    )
    outputs = call(
        unpack_last,
        "unpack_last",
        shape(patches, frames, local, width),
        (patch_frames,),
        (swap(sent),),
        [pltpu.VMEM((ticks * owned + SUBLANES, width), jnp.float32)],
    )
    return outputs[None]


def solution(mesh):
    in_specs = (
        P("section", None, "seq", None),
        P(None, None, "seq", None),
        P(),
        P("section", None),
        P("section", None, None, "seq"),
        P("section", None, "seq"),
        P("section", None, None, None, None, "seq"),
    )
    out_specs = P("section", None, None, "seq", None)
    return jax.shard_map(
        on_device, mesh=mesh, in_specs=in_specs, out_specs=out_specs, check_vma=False
    )
```

```python
import functools
import math

import jax
import jax.numpy as jnp
from jax import lax
from jax.experimental import pallas as pl
from jax.experimental.pallas import tpu as pltpu
from jax.sharding import PartitionSpec as P

HDIM = 128
CORES = 2
WEIGHT_PARTS = 4
SUBLANES = 8
MOST_SECTIONS = 1024
VMEM_LIMIT = 12 * 1024 * 1024


def call(body, name, out_shape, scalars, arrays, scratch=(), in_hbm=(), aliases=()):
    arrays = [
        pltpu.with_memory_space_constraint(array, pltpu.HBM) if place in in_hbm else array
        for place, array in enumerate(arrays)
    ]
    in_vmem = pl.BlockSpec(memory_space=pltpu.VMEM)
    in_smem = pl.BlockSpec(memory_space=pltpu.SMEM)
    return pl.pallas_call(
        body,
        out_shape=out_shape,
        in_specs=[in_smem] * len(scalars)
        + [pl.BlockSpec(memory_space=pl.ANY) if place in in_hbm else in_vmem for place in range(len(arrays))],
        out_specs=jax.tree.map(lambda _: in_vmem, out_shape),
        scratch_shapes=list(scratch),
        input_output_aliases=dict(aliases),
        compiler_params=pltpu.CompilerParams(vmem_limit_bytes=VMEM_LIMIT),
        name=name,
    )(*scalars, *arrays)


def shape(*dims):
    return jax.ShapeDtypeStruct(dims, jnp.bfloat16)


def fetch_rows(tokens_any, tokens_ref, rows_ref, sem_ref):
    fetch = pltpu.make_async_copy(tokens_any, tokens_ref, sem_ref.at[0])
    fetch.start()
    fetch.wait()
    frames, local, width = tokens_ref.shape
    blocks = width // HDIM
    for frame in range(frames):
        wide = tokens_ref[frame].astype(jnp.float32)
        for block in range(blocks):
            rows_ref[pl.ds(frame * local * blocks + block, local, stride=blocks), :] = wide[
                :, block * HDIM:(block + 1) * HDIM
            ]


def send_rows(rows_ref, out_ref):
    chips, halves, tokens, _ = out_ref.shape
    for half in range(halves):
        rows = rows_ref[half * tokens:(half + 1) * tokens].astype(jnp.bfloat16)
        for chip in range(chips):
            out_ref[chip, half] = rows


def pack_first(mine_any, out_ref, mine_ref, rows_ref, sem_ref):
    fetch_rows(mine_any.at[0], mine_ref, rows_ref, sem_ref)
    send_rows(rows_ref, out_ref)


def to_blocks(came_ref, hidden_ref, wide_ref):
    chips, halves, tokens, _ = came_ref.shape
    blocks = chips * halves
    for chip in range(chips):
        for half in range(halves):
            first = (chip * halves + half) * tokens
            wide_ref[first:first + tokens] = came_ref[chip, half].astype(jnp.float32)
    for token in range(tokens // chips):
        for block in range(blocks):
            hidden_ref[block // halves, block % halves, token * chips:(token + 1) * chips] = wide_ref[
                pl.ds(token * blocks + block, chips, stride=halves * tokens), :
            ].astype(jnp.bfloat16)


def spread(tick, entering_any, arrived_ref, out_ref, tokens_ref, rows_ref, sem_ref):
    section = lax.axis_index("section")

    @pl.when(section == 0)
    def _():
        fetch_rows(entering_any.at[tick - 1], tokens_ref, rows_ref, sem_ref)
        send_rows(rows_ref, out_ref)

    @pl.when(section != 0)
    def _():
        for chip in range(out_ref.shape[0]):
            out_ref[chip] = arrived_ref[...]


def arrange(came_ref, hidden_ref, wide_ref):
    @pl.when(lax.axis_index("section") == 0)
    def _():
        to_blocks(came_ref, hidden_ref, wide_ref)


def slot_of(frames_ref, tick):
    slots = frames_ref.shape[0]
    return lax.rem(tick + slots * MOST_SECTIONS - lax.axis_index("section"), slots)


def own_core():
    return lax.rem(lax.axis_index("seq"), CORES)


def live_rows(frames, frames_ref, tick, rows):
    row_ids = lax.broadcasted_iota(jnp.int32, (rows, 1), 0)
    return row_ids < frames_ref[slot_of(frames_ref, tick)] * (rows // frames)


def first_rows(tokens, slot_rows, width):
    stale = tokens + slot_rows // CORES
    return stale, stale + width // WEIGHT_PARTS


def two_heads(own_ref, other_ref, kinds, span):
    return jnp.concatenate([ref[kind, span] for ref in (own_ref, other_ref) for kind in kinds], axis=1)


def layer_keys_first(
    frames, frames_any, came_ref, gain_any, w_own_any, w_other_ref, weight_any, stale_any,
    x_ref, w_own_ref, weight_ref, xn_ref, new_ref, stale_ref, wide_ref, frames_ref, gain_ref, sem_ref,
):
    firsts = [
        pltpu.make_async_copy(frames_any, frames_ref, sem_ref.at[2]),
        pltpu.make_async_copy(gain_any, gain_ref, sem_ref.at[3]),
        pltpu.make_async_copy(w_own_any, w_own_ref, sem_ref.at[4]),
    ]
    for first in firsts:
        first.start()
    fetches = [
        pltpu.make_async_copy(weight_any, weight_ref, sem_ref.at[0]),
        pltpu.make_async_copy(stale_any, stale_ref, sem_ref.at[1]),
    ]
    for fetch in fetches:
        fetch.start()
    to_blocks(came_ref, x_ref, wide_ref)
    for first in firsts:
        first.wait()
    layer_keys(
        0, frames, frames_ref, x_ref, gain_ref, w_own_ref, w_other_ref,
        stale_ref, weight_ref, xn_ref, new_ref, wide_ref, fetches=fetches,
    )


def layer_keys(tick, frames, frames_ref, x_ref, gain_ref, w_own_ref, w_other_ref, *refs, fetches=()):
    *first_refs, xn_ref, new_ref = refs if tick else refs[:-1]
    chips, halves, tokens, width = x_ref.shape
    pair = halves * width
    squares = jnp.zeros((tokens, width), jnp.float32)
    for chip in range(chips):
        for half in range(halves):
            wide = x_ref[chip, half].astype(jnp.float32)
            squares = squares + wide * wide
    mean_square = jnp.sum(squares, axis=1, keepdims=True) / (chips * pair)
    scale = jnp.where(live_rows(frames, frames_ref, tick, tokens), lax.rsqrt(mean_square + 1e-06), 0.0)
    total = jnp.zeros((tokens, 2 * pair), jnp.float32)
    for chip in range(chips):
        span = slice(chip * pair, (chip + 1) * pair)
        wide = jnp.concatenate([x_ref[chip, half] for half in range(halves)], axis=1).astype(jnp.float32)
        normed = (wide * scale * gain_ref[:, span].astype(jnp.float32)).astype(jnp.bfloat16)
        xn_ref[:, span] = normed
        total = total + jnp.dot(
            normed, two_heads(w_own_ref, w_other_ref, (1, 2), span), preferred_element_type=jnp.float32
        )
    new_ref[:tokens] = total.astype(jnp.bfloat16)
    if tick == 0:
        stale_ref, out_ref = first_refs
        wide_ref = refs[-1].at[:stale_ref.shape[0]]
        for fetch in fetches:
            fetch.wait()
        rows = stale_ref.shape[0] // 2
        stale_end, weight_end = first_rows(tokens, rows, out_ref.shape[0])
        wide_ref[...] = stale_ref[...].astype(jnp.float32)
        each = rows // CORES
        for part in range(CORES):
            for kind in range(2):
                first = (part * 2 + kind) * width
                new_ref[tokens:stale_end, first:first + width] = wide_ref[
                    pl.ds(part * 2 * each + kind, each, stride=2), :
                ].astype(jnp.bfloat16)
        part_rows = weight_end - stale_end
        for part in range(WEIGHT_PARTS):
            new_ref[stale_end:weight_end, part * width:(part + 1) * width] = out_ref[
                part * part_rows:(part + 1) * part_rows
            ]


def layer_queries(xn_ref, w_own_ref, w_other_ref, out_ref):
    pair = out_ref.shape[1]
    total = jnp.zeros(out_ref.shape, jnp.float32)
    for first in range(0, xn_ref.shape[1], pair):
        span = slice(first, first + pair)
        total = total + jnp.dot(
            xn_ref[:, span], two_heads(w_own_ref, w_other_ref, (0,), span), preferred_element_type=jnp.float32
        )
    out_ref[...] = total.astype(jnp.bfloat16)


def layer_attend(tick, frames, frames_ref, q_ref, own_ref, other_ref, *refs):
    out_ref, kv_out = refs[-2:]
    chips, halves, tokens, width = out_ref.shape
    slots = kv_out.shape[0]
    rows = CORES * tokens
    span = tokens // frames
    both = 2 * width
    slot = slot_of(frames_ref, tick)
    core = own_core()
    if tick == 0:
        for place_of, ref in enumerate((own_ref, other_ref)):
            columns = slice(place_of * both, (place_of + 1) * both)
            for old in range(slots):
                part, place = divmod(old, slots // CORES)
                for frame in range(frames):
                    for piece in range(CORES):
                        row = tokens + place * rows + (frame * CORES + piece) * span
                        kv_out[old, piece, frame * span:(frame + 1) * span, columns] = ref[
                            row:row + span, part * both:(part + 1) * both
                        ]
    kv_out[slot, core] = own_ref[:tokens]
    kv_out[slot, 1 - core, :, :both] = other_ref[:tokens, both:]
    kv_out[slot, 1 - core, :, both:] = other_ref[:tokens, :both]
    key_ids = lax.broadcasted_iota(jnp.int32, (1, slots * rows), 1)
    limit = jnp.zeros_like(key_ids)
    for patch in range(slots):
        limit = jnp.where(key_ids // rows == patch, frames_ref[patch] * span, limit)
    key_live = key_ids % tokens < limit
    scores = []
    for head in range(halves):
        keys = kv_out[:, :, :, head * both:head * both + width].reshape(slots * rows, width)
        scores.append(
            lax.dot_general(
                q_ref[:, head * width:(head + 1) * width], keys, (((1,), (1,)), ((), ())),
                preferred_element_type=jnp.float32,
            )
        )
    scores = jnp.where(key_live, jnp.concatenate(scores, axis=0) * (1.0 / math.sqrt(HDIM)), -jnp.inf)
    exponent = jnp.exp(scores - jnp.max(scores, axis=1, keepdims=True))
    weights_low = exponent.astype(jnp.bfloat16)
    share = 1.0 / jnp.sum(exponent, axis=1, keepdims=True)
    attended = []
    for head in range(halves):
        span = slice(head * tokens, (head + 1) * tokens)
        values = kv_out[:, :, :, head * both + width:(head + 1) * both].reshape(slots * rows, width)
        weighted = jnp.dot(weights_low[span], values, preferred_element_type=jnp.float32)
        attended.append((weighted * share[span]).astype(jnp.bfloat16))
    for head, half in enumerate((core, 1 - core)):
        for chip in range(chips):
            out_ref[chip, half] = attended[head]


def layer_back(tick, frames, slot_rows, frames_ref, a_ref, w_own_ref, first_other_ref, x_ref, out_ref):
    chips, halves, tokens, width = a_ref.shape
    pair = halves * width
    chip = lax.div(lax.axis_index("seq"), CORES)
    core = own_core()
    live = live_rows(frames, frames_ref, tick, tokens)
    stale_end, weight_end = first_rows(tokens, slot_rows, w_own_ref.shape[0])
    branch = jnp.zeros((tokens, pair), jnp.float32)
    for source in range(chips):
        wide = jnp.concatenate([a_ref[source, half] for half in range(halves)], axis=1)
        part, row = divmod(source * pair, weight_end - stale_end)
        row += stale_end
        weights = jnp.concatenate(
            [
                w_own_ref[source * pair:(source + 1) * pair],
                first_other_ref[row:row + pair, part * width:(part + 1) * width],
            ],
            axis=1,
        )
        branch = branch + jnp.dot(wide, weights, preferred_element_type=jnp.float32)
    branch = branch.astype(jnp.bfloat16).astype(jnp.float32)
    for head, half in enumerate((core, 1 - core)):
        total = x_ref[chip, half].astype(jnp.float32) + branch[:, head * width:(head + 1) * width]
        out_ref[half] = jnp.where(live, total, 0.0).astype(jnp.bfloat16)


def pack_last(*refs):
    *result_refs, out_ref, wide_ref = refs
    chips, parts, _ = out_ref.shape
    ticks = len(result_refs)
    for tick, ref in enumerate(result_refs):
        halves, tokens, _ = ref.shape
        for half in range(halves):
            first = (half * ticks + tick) * tokens
            wide_ref[first:first + tokens] = ref[half].astype(jnp.float32)
    for chip in range(chips):
        out_ref[chip] = wide_ref[pl.ds(chip, parts, stride=chips), :].astype(jnp.bfloat16)


def unpack_last(frames_ref, came_ref, out_ref, turn_ref):
    chips, parts, width = came_ref.shape
    patches, frames, local, _ = out_ref.shape
    each = parts // CORES
    for chip in range(chips):
        wide = came_ref[chip].astype(jnp.float32)
        for half in range(CORES):
            first = (chip * CORES + half) * width
            turn_ref[:each, first:first + width] = wide[half * each:(half + 1) * each]
    for tick in range(patches):
        slot = slot_of(frames_ref, tick)
        for frame in range(frames):
            row = (tick * frames + frame) * local
            out_ref[slot, frame] = turn_ref[row:row + local].astype(jnp.bfloat16)


def on_device(in_flight, entering, patch_frames, norm_gain, qkv_weight, out_weight, stale_kv):
    sections = lax.axis_size("section")
    group = lax.axis_size("seq")
    patches, frames, tokens = stale_kv.shape[1:4]
    local = in_flight.shape[2]
    width = in_flight.shape[3]
    ticks = patches
    chips = group // CORES
    halves = CORES
    owned = frames * local
    rows = owned * chips
    blocks = chips * halves
    same_core = [[CORES * chip + core for chip in range(chips)] for core in range(CORES)]
    partner = [(device, device ^ 1) for device in range(group)]

    def swap(value):
        return lax.all_to_all(
            value, "seq", split_axis=0, concat_axis=0, tiled=True, axis_index_groups=same_core
        )

    w_in = jnp.transpose(qkv_weight[0], (1, 0, 2))
    w_in_other = lax.ppermute(w_in, "seq", partner)
    stale = stale_kv[0].reshape(patches * frames * tokens * 2, HDIM)
    block_dims = (chips, halves, rows, HDIM)
    token_scratch = [
        pltpu.VMEM((frames, local, width), jnp.bfloat16),
        pltpu.VMEM(((owned + SUBLANES) * blocks, HDIM), jnp.float32),
        pltpu.SemaphoreType.DMA((1,)),
    ]
    wide = pltpu.VMEM((chips * halves * rows, HDIM), jnp.float32)
    came = swap(call(pack_first, "pack_first", shape(*block_dims), (), (in_flight,), token_scratch, in_hbm=(0,)))
    results = []
    for tick in range(ticks):
        if tick:
            arrived = lax.ppermute(
                results[-1], "section", [(source, source + 1) for source in range(sections - 1)]
            )
            sent = call(
                functools.partial(spread, tick),
                "spread",
                shape(*block_dims),
                (),
                (entering, arrived),
                token_scratch,
                in_hbm=(0,),
            )
            gathered = call(arrange, "arrange", shape(*block_dims), (), (swap(sent),), [wide], aliases={0: 0})
        new_rows = rows if tick else first_rows(rows, stale.shape[0] // 2, width)[1]
        if tick == 0:
            gathered, w_in, w_out, normed, own = call(
                functools.partial(layer_keys_first, frames),
                "keys_first",
                (
                    shape(*block_dims),
                    shape(*w_in.shape),
                    shape(width, HDIM),
                    shape(rows, width),
                    shape(new_rows, 2 * halves * HDIM),
                ),
                (),
                (patch_frames, came, norm_gain, w_in, w_in_other, out_weight[0], stale),
                [
                    pltpu.VMEM(stale.shape, jnp.bfloat16),
                    wide,
                    pltpu.SMEM(patch_frames.shape, jnp.int32),
                    pltpu.VMEM(norm_gain.shape, jnp.bfloat16),
                    pltpu.SemaphoreType.DMA((5,)),
                ],
                in_hbm=(0, 2, 3, 5, 6),
            )
        else:
            normed, own = call(
                functools.partial(layer_keys, tick, frames),
                "keys",
                (shape(rows, width), shape(new_rows, 2 * halves * HDIM)),
                (patch_frames,),
                (gathered, norm_gain, w_in, w_in_other),
            )
        other = lax.ppermute(own, "seq", partner)
        queries = call(layer_queries, "queries", shape(rows, halves * HDIM), (), (normed, w_in, w_in_other))
        attended, kv = call(
            functools.partial(layer_attend, tick, frames),
            "attend",
            (shape(chips, halves, rows, HDIM), shape(patches, CORES, rows, 2 * halves * HDIM)),
            (patch_frames,),
            (queries, own, other) + ((kv,) if tick else ()),
            aliases={4: 1} if tick else {},
        )
        if tick == 0:
            first_other = other
        results.append(
            call(
                functools.partial(layer_back, tick, frames, stale.shape[0] // 2),
                "back",
                shape(halves, rows, HDIM),
                (patch_frames,),
                (swap(attended), w_out, first_other, gathered),
            )
        )

    parts = ticks * halves * owned
    sent = call(
        pack_last,
        "pack_last",
        shape(chips, parts, HDIM),
        (),
        tuple(results),
        [pltpu.VMEM((ticks * halves * rows, HDIM), jnp.float32)],
    )
    outputs = call(
        unpack_last,
        "unpack_last",
        shape(patches, frames, local, width),
        (patch_frames,),
        (swap(sent),),
        [pltpu.VMEM((ticks * owned + SUBLANES, width), jnp.float32)],
    )
    return outputs[None]


def solution(mesh):
    in_specs = (
        P("section", None, "seq", None),
        P(None, None, "seq", None),
        P(),
        P("section", None),
        P("section", None, None, "seq"),
        P("section", None, "seq"),
        P("section", None, None, None, None, "seq"),
    )
    out_specs = P("section", None, None, "seq", None)
    return jax.shard_map(
        on_device, mesh=mesh, in_specs=in_specs, out_specs=out_specs, check_vma=False
    )
```
